256 devices in a mesh: seq: 128 (over y_hi, z, x, core), ch: 2 (over y_lo).
Axes of the slice: x: 4, y: 4 (y_hi: 2, y_lo: 2; y = y_hi * 2 + y_lo), z: 8, core: 2. Of those that a mesh axis runs over, the one named last changes fastest.
Arguments:
- features: bfloat16 [131072, 4096], P('seq', 'ch'), may hold values from -6 to 6
- value_weight: bfloat16 [4096, 512], P('ch'), may hold values from -0.09375 to 0.09375
- gate_weight: bfloat16 [4096, 512], P('ch'), may hold values from -0.09375 to 0.09375
- kernel: bfloat16 [1024, 512], P('seq', 'ch'), may hold values from -0.5 to 0.5
- skip_gain: float32 [512], P('ch'), may hold values from 0.5 to 1.5
Outputs:
- mixed: bfloat16 [131072, 512], P('seq', 'ch')
The draws below stay inside these ranges and needn't reach their ends.
All inputs are finite; a program needn't handle non-finite values.
Results may differ from the reference program's by a relative error of at most 0.0049.
Values may be sent and summed in bfloat16 or wider, within the bound.
A program may use at most 128 MiB of HBM per device.

```python
import jax
import jax.numpy as jnp

D = 4096
G = 512
TOK_DEV = 1024
TOKENS = 131072
KLEN = 1024


def block_scale(own_key, dims, cuts, low, high):
    gain, own = 1.0, jax.random.fold_in(own_key, 6)
    for position, blocks in cuts:
        steps = jnp.exp(jax.random.uniform(jax.random.fold_in(own, position), (blocks,), jnp.float32, low / len(cuts), high / len(cuts)))
        gain = gain * jnp.repeat(steps, dims[position] // blocks).reshape([-1 if axis == position else 1 for axis in range(len(dims))])
    return gain


def scatter_about(key, shape, deviation, limit, split=(), kind=jnp.bfloat16):
    array = deviation * jax.random.normal(key, shape, jnp.float32)
    if split:
        array = array * block_scale(key, shape, split, -0.22, 0.18)
    return jnp.clip(array, -limit, limit).astype(kind)


def setup_inputs(seed: int = 0) -> dict:
    keys = jax.random.split(jax.random.key(seed), 6)
    features = scatter_about(keys[0], (TOKENS, D), 1.0, 6.0, ((0, 128), (1, 2)))
    value_weight = scatter_about(keys[1], (D, G), D ** -0.5, 0.09375, ((0, 2),))
    gate_weight = scatter_about(keys[2], (D, G), D ** -0.5, 0.09375, ((0, 2),))
    kernel = scatter_about(keys[3], (KLEN, G), (TOK_DEV ** -0.5), 0.5, ((0, 128), (1, 2)))
    skip_gain = jnp.clip(0.5 + 1.0 * jax.random.uniform(keys[4], (G,), jnp.float32) ** block_scale(keys[4], (G,), ((0, 2),), -0.2, 0.2), 0.5, 1.5)
    return {"features": features, "value_weight": value_weight, "gate_weight": gate_weight, "kernel": kernel, "skip_gain": skip_gain}


def reference(features, value_weight, gate_weight, kernel, skip_gain):
    projected = jnp.dot(features, value_weight, preferred_element_type=jnp.float32).astype(jnp.bfloat16)
    gate_sum = jnp.dot(features, gate_weight, preferred_element_type=jnp.float32)
    length = 1 << (TOKENS + KLEN - 1).bit_length()
    values_wide = projected.astype(jnp.float32)
    kernel_wide = kernel.astype(jnp.float32)
    spectrum = jnp.fft.rfft(values_wide, length, axis=0) * jnp.fft.rfft(kernel_wide, length, axis=0)
    convolved = jnp.fft.irfft(spectrum, length, axis=0)[:TOKENS].astype(jnp.float32)
    mixed = (convolved + skip_gain[None, :] * values_wide) * jax.nn.silu(gate_sum)
    return mixed.astype(jnp.bfloat16)
```

```python
import functools
import math

import jax
import jax.numpy as jnp
import numpy as np
from jax import lax
from jax.experimental import pallas as pl
from jax.experimental.pallas import tpu as pltpu
from jax.sharding import PartitionSpec as P

MESH = pl.DeviceIdType.MESH
WIRE = jnp.bfloat16
GRID = (2, 8, 4, 2)
BLOCKS = 8
CHUNKS = 4


def split_bf16(table):
    high = table.astype(np.float32).astype(jnp.bfloat16)
    low = (table - high.astype(np.float64)).astype(np.float32).astype(jnp.bfloat16)
    return np.stack([high, low])


def tables(block, seqs):
    period = 2 * block
    freq = np.arange(block)[:, None] + 0.5
    place = np.arange(period)[None, :]
    phase = 2.0 * math.pi * freq * place / period
    forward = np.concatenate([np.cos(phase), np.sin(phase)], 0)
    inverse = forward.T[block:] * (2.0 / period)
    taps = np.zeros((2, period, seqs, 2, 8))
    for half in range(2):
        taps[half, :, :, half, :] = forward[:, :block].reshape(period, seqs, 8)
    return (
        split_bf16(forward),
        split_bf16(taps.reshape(2 * period, seqs * 16)),
        split_bf16(inverse),
    )


def layer(
    grid,
    blocks,
    chunks,
    feat_hbm,
    vw_hbm,
    gw_hbm,
    ker_hbm,
    skip_hbm,
    fwd_hbm,
    fker_hbm,
    inv_hbm,
    out_hbm,
    feat,
    wgt,
    ktmp,
    skip,
    fwd,
    fker,
    inv,
    kg,
    vsend,
    vrecv,
    gsend,
    grecv,
    vown,
    gown,
    xs,
    es,
    kh,
    ys,
    conv,
    obuf,
    in_sem,
    feat_sem,
    out_sem,
    v_ssem,
    v_rsem,
    g_ssem,
    g_rsem,
    h_ssem,
    h_rsem,
    a_sem,
    z_ssem,
    z_rsem,
    x_ssem,
    x_rsem,
    c_sem,
):
    n_yh, n_z, n_x, n_core = grid
    n_seq = n_yh * n_z * n_x * n_core
    rows = feat.shape[0]
    size = rows // chunks
    block = rows // blocks
    channels = vown.shape[1]
    seqs = n_seq // blocks

    me = lax.axis_index("seq")
    side = lax.axis_index("ch")
    core = me % n_core
    x = me // n_core % n_x
    z = me // (n_core * n_x) % n_z
    yh = me // (n_core * n_x * n_z)

    def seq_of(yh, z, x, core):
        return ((yh * n_z + z) * n_x + x) * n_core + core

    other = pl.ds(pl.multiple_of((1 - side) * channels, 128), channels)
    own = pl.ds(pl.multiple_of(side * channels, 128), channels)

    def feat_copy(i):
        part = pl.ds(pl.multiple_of(i * size, size), size)
        return pltpu.make_async_copy(feat_hbm.at[part], feat.at[part], feat_sem.at[i])

    weight_copies = [
        pltpu.make_async_copy(hbm.at[:, cols], wgt.at[j], in_sem.at[j])
        for j, (hbm, cols) in enumerate(
            ((vw_hbm, other), (vw_hbm, own), (gw_hbm, other), (gw_hbm, own))
        )
    ]
    small_copies = [
        pltpu.make_async_copy(hbm, ref, in_sem.at[4 + j])
        for j, (hbm, ref) in enumerate(
            (
                (ker_hbm, ktmp),
                (fker_hbm, fker),
                (fwd_hbm, fwd),
                (inv_hbm, inv),
                (skip_hbm, skip),
            )
        )
    ]
    small_copies[0].start()
    feat_copy(0).start()
    weight_copies[0].start()
    for i in range(1, chunks):
        feat_copy(i).start()
    for copy in weight_copies[1:]:
        copy.start()
    for copy in small_copies[1:]:
        copy.start()

    partner = {"ch": 1 - side}
    following = {"seq": (me + 1) % n_seq}
    preceding = {"seq": (me + n_seq - 1) % n_seq}
    yh_partner = {"seq": seq_of(1 - yh, z, x, core)}
    core_partner = {"seq": seq_of(yh, z, x, 1 - core)}
    z_to = {d: {"seq": seq_of(yh, (z + d) % n_z, x, core)} for d in range(1, n_z)}
    x_to = {d: {"seq": seq_of(yh, z, (x + d) % n_x, core)} for d in range(1, n_x)}
    everyone = [partner, following, preceding, yh_partner, core_partner]
    everyone += list(z_to.values()) + list(x_to.values())
    barrier = pltpu.get_barrier_semaphore()
    for device in everyone:
        pl.semaphore_signal(barrier, inc=1, device_id=device, device_id_type=MESH)

    def remote(src, dst, ssem, rsem, device):
        return pltpu.make_async_remote_copy(
            src_ref=src,
            dst_ref=dst,
            send_sem=ssem,
            recv_sem=rsem,
            device_id=device,
            device_id_type=MESH,
        )

    def part(i):
        return pl.ds(pl.multiple_of(i * size, size), size)

    def v_copy(i):
        return remote(vsend.at[part(i)], vrecv.at[part(i)], v_ssem.at[i], v_rsem.at[i], partner)

    def g_copy(i):
        return remote(gsend.at[part(i)], grecv.at[part(i)], g_ssem.at[i], g_rsem.at[i], partner)

    def current(i):
        return pl.ds(pl.multiple_of(rows + i * size, size), size)

    def h_copy(i):
        return remote(xs.at[current(i)], xs.at[part(i)], h_ssem.at[i], h_rsem.at[i], following)

    def a_copy(sender):
        slot = kg.at[core, x, z, sender]
        return remote(slot, slot, a_sem.at[0], a_sem.at[1], yh_partner)

    def z_copy(d, sender):
        slot = kg.at[core, x, sender]
        return remote(slot, slot, z_ssem.at[d], z_rsem.at[d], z_to[d])

    def x_copy(d, sender):
        slot = kg.at[core, sender]
        return remote(slot, slot, x_ssem.at[d], x_rsem.at[d], x_to[d])

    def c_copy(sender):
        slot = kg.at[sender]
        return remote(slot, slot, c_sem.at[0], c_sem.at[1], core_partner)

    small_copies[0].wait()
    taps = ktmp[...].astype(jnp.float32)
    half = channels // 2
    kg[core, x, z, yh] = jnp.concatenate([taps[:, :half], taps[:, half:]], 0).astype(kg.dtype)

    weight_copies[0].wait()

    @pl.loop(0, chunks)
    def _(i):
        feat_copy(i).wait()
        total = jnp.dot(feat[part(i)], wgt[0], preferred_element_type=jnp.float32)
        vsend[part(i)] = total.astype(vsend.dtype)

        @pl.when(i == 0)
        def _():
            pl.semaphore_wait(barrier, len(everyone))
            a_copy(yh).start()

        v_copy(i).start()

    a_copy(1 - yh).wait_recv()
    for d in range(1, n_z):
        z_copy(d, z).start()

    weight_copies[1].wait()

    @pl.loop(0, chunks)
    def _(i):
        vown[part(i)] = jnp.dot(feat[part(i)], wgt[1], preferred_element_type=jnp.float32)

    for d in range(1, n_z):
        z_copy(d, (z + n_z - d) % n_z).wait_recv()
    for d in range(1, n_x):
        x_copy(d, x).start()

    weight_copies[2].wait()

    @pl.loop(0, chunks)
    def _(i):
        total = jnp.dot(feat[part(i)], wgt[2], preferred_element_type=jnp.float32)
        gsend[part(i)] = total.astype(gsend.dtype)

    weight_copies[3].wait()

    @pl.loop(0, chunks)
    def _(i):
        gown[part(i)] = jnp.dot(feat[part(i)], wgt[3], preferred_element_type=jnp.float32)

    for d in range(1, n_x):
        x_copy(d, (x + n_x - d) % n_x).wait_recv()
    c_copy(core).start()

    @pl.loop(0, chunks)
    def _(i):
        v_copy(i).wait_recv()
        total = vown[part(i)] + vrecv[part(i)].astype(jnp.float32)
        xs[current(i)] = total.astype(xs.dtype)

        @pl.when(me < n_seq - 1)
        def _():
            h_copy(i).start()

        @pl.when(i == chunks - 2)
        def _():
            g_copy(0).start()

    for i in range(1, chunks):
        g_copy(i).start()

    c_copy(1 - core).wait_recv()
    for copy in small_copies[1:]:
        copy.wait()
    for p in range(blocks):
        pieces = []
        for seq in range(p * seqs, (p + 1) * seqs):
            at_core, at_x = seq % n_core, seq // n_core % n_x
            at_z, at_yh = seq // (n_core * n_x) % n_z, seq // (n_core * n_x * n_z)
            pieces.append(kg[at_core, at_x, at_z, at_yh])
        taps = jnp.concatenate(pieces, 0)
        kh[p] = jnp.dot(fker[0], taps, preferred_element_type=jnp.float32) + jnp.dot(
            fker[1], taps, preferred_element_type=jnp.float32
        )

    def forward(m):
        pair = xs[pl.ds(pl.multiple_of(m * block, block), 2 * block)]
        es[m] = jnp.dot(fwd[0], pair, preferred_element_type=jnp.float32) + jnp.dot(
            fwd[1], pair, preferred_element_type=jnp.float32
        )

    pl.loop(blocks, 2 * blocks - 1)(forward)

    @pl.when(me == 0)
    def _():
        xs[pl.ds(0, rows)] = jnp.zeros((rows, channels), xs.dtype)

    @pl.when(me > 0)
    def _():
        for i in range(chunks):
            h_copy(i).wait_recv()

    pl.loop(0, blocks)(forward)

    @pl.loop(0, block // 8)
    def _(r):
        real = pl.ds(pl.multiple_of(r * 8, 8), 8)
        imag = pl.ds(pl.multiple_of(block + r * 8, 8), 8)
        for part_of in range(2):
            lanes = pl.ds(part_of * half, half)
            at = part_of * 2 * block
            k_real = [kh[p, pl.ds(pl.multiple_of(at + r * 8, 8), 8)] for p in range(blocks)]
            k_imag = [kh[p, pl.ds(pl.multiple_of(at + block + r * 8, 8), 8)] for p in range(blocks)]
            sum_real = [None] * blocks
            sum_imag = [None] * blocks
            for m in range(2 * blocks - 1):
                e_real, e_imag = es[m, real, lanes], es[m, imag, lanes]
                for a in range(blocks):
                    p = blocks - 1 + a - m
                    if not 0 <= p < blocks:
                        continue
                    new_real = e_real * k_real[p] - e_imag * k_imag[p]
                    new_imag = e_imag * k_real[p] + e_real * k_imag[p]
                    if sum_real[a] is None:
                        sum_real[a], sum_imag[a] = new_real, new_imag
                    else:
                        sum_real[a], sum_imag[a] = sum_real[a] + new_real, sum_imag[a] + new_imag
            for a in range(blocks):
                ys[a, real, lanes] = sum_real[a]
                ys[a, imag, lanes] = sum_imag[a]

    gain = skip[...]

    @pl.loop(0, blocks)
    def _(a):
        spectrum = ys[a]
        high = spectrum.astype(jnp.bfloat16)
        low = (spectrum - high.astype(jnp.float32)).astype(jnp.bfloat16)
        back = (
            jnp.dot(inv[0], high, preferred_element_type=jnp.float32)
            + jnp.dot(inv[1], high, preferred_element_type=jnp.float32)
            + jnp.dot(inv[0], low, preferred_element_type=jnp.float32)
        )
        direct = xs[pl.ds(pl.multiple_of(rows + a * block, block), block)].astype(jnp.float32)
        conv[pl.ds(pl.multiple_of(a * block, block), block)] = back + gain * direct

    def out_copy(i):
        return pltpu.make_async_copy(obuf.at[part(i)], out_hbm.at[part(i)], out_sem.at[i])

    @pl.loop(0, chunks)
    def _(i):
        g_copy(i).wait_recv()
        gate = gown[part(i)] + grecv[part(i)].astype(jnp.float32)
        obuf[part(i)] = (conv[part(i)] * (gate / (1.0 + jnp.exp(-gate)))).astype(obuf.dtype)
        out_copy(i).start()

    for i in range(chunks):
        v_copy(i).wait_send()
        g_copy(i).wait_send()

    @pl.when(me < n_seq - 1)
    def _():
        for i in range(chunks):
            h_copy(i).wait_send()

    a_copy(yh).wait_send()
    for d in range(1, n_z):
        z_copy(d, z).wait_send()
    for d in range(1, n_x):
        x_copy(d, x).wait_send()
    c_copy(core).wait_send()
    for i in range(chunks):
        out_copy(i).wait()


def solution(mesh, grid=GRID, blocks=BLOCKS, chunks=CHUNKS):
    def on_device(features, value_weight, gate_weight, kernel, skip_gain):
        rows, depth = features.shape
        tap_rows, channels = kernel.shape
        n_seq = math.prod(grid)
        block = rows // blocks
        seqs = n_seq // blocks
        fwd, fker, inv = tables(block, seqs)
        f32, bf16 = jnp.float32, jnp.bfloat16
        dma = pltpu.SemaphoreType.DMA
        n_yh, n_z, n_x, n_core = grid
        return pl.pallas_call(
            functools.partial(layer, grid, blocks, chunks),
            out_shape=jax.ShapeDtypeStruct((rows, channels), bf16),
            in_specs=[pl.BlockSpec(memory_space=pl.ANY)] * 8,
            out_specs=pl.BlockSpec(memory_space=pl.ANY),
            scratch_shapes=[
                pltpu.VMEM((rows, depth), bf16),
                pltpu.VMEM((4, depth, channels), bf16),
                pltpu.VMEM((tap_rows, channels), bf16),
                pltpu.VMEM((1, channels), f32),
                pltpu.VMEM(fwd.shape, bf16),
                pltpu.VMEM(fker.shape, bf16),
                pltpu.VMEM(inv.shape, bf16),
                pltpu.VMEM((n_core, n_x, n_z, n_yh, 2 * tap_rows, channels // 2), bf16),
                pltpu.VMEM((rows, channels), WIRE),
                pltpu.VMEM((rows, channels), WIRE),
                pltpu.VMEM((rows, channels), WIRE),
                pltpu.VMEM((rows, channels), WIRE),
                pltpu.VMEM((rows, channels), f32),
                pltpu.VMEM((rows, channels), f32),
                pltpu.VMEM((2 * rows, channels), bf16),
                pltpu.VMEM((2 * blocks - 1, 2 * block, channels), f32),
                pltpu.VMEM((blocks, 4 * block, channels // 2), f32),
                pltpu.VMEM((blocks, 2 * block, channels), f32),
                pltpu.VMEM((rows, channels), f32),
                pltpu.VMEM((rows, channels), bf16),
                dma((9,)),
                dma((chunks,)),
                dma((chunks,)),
                dma((chunks,)),
                dma((chunks,)),
                dma((chunks,)),
                dma((chunks,)),
                dma((chunks,)),
                dma((chunks,)),
                dma((2,)),
                dma((n_z,)),
                dma((n_z,)),
                dma((n_x,)),
                dma((n_x,)),
                dma((2,)),
            ],
            compiler_params=pltpu.CompilerParams(
                collective_id=0, has_side_effects=True, vmem_limit_bytes=56 * 2**20
            ),
            cost_estimate=pl.CostEstimate(
                flops=8 * rows * depth * channels,
                bytes_accessed=2 * (rows * depth + 4 * depth * channels + rows * channels),
                transcendentals=rows * channels,
            ),
        )(
            features,
            value_weight,
            gate_weight,
            kernel,
            skip_gain.reshape(1, channels),
            jnp.asarray(fwd),
            jnp.asarray(fker),
            jnp.asarray(inv),
        )

    return jax.shard_map(
        on_device,
        mesh=mesh,
        in_specs=(P("seq", "ch"), P("ch", None), P("ch", None), P("seq", "ch"), P("ch")),
        out_specs=P("seq", "ch"),
        check_vma=False,
    )
```

```python
import functools
import math

import jax
import jax.numpy as jnp
import numpy as np
from jax import lax
from jax.experimental import pallas as pl
from jax.experimental.pallas import tpu as pltpu
from jax.sharding import PartitionSpec as P

MESH = pl.DeviceIdType.MESH
WIRE = jnp.bfloat16
GRID = (2, 8, 4, 2)
BLOCKS = 8
CHUNKS = 4


def tables(block):
    period = 2 * block
    freq = np.arange(block)[:, None] + 0.5
    place = np.arange(period)[None, :]
    phase = 2.0 * math.pi * freq * place / period
    forward = np.concatenate([np.cos(phase), np.sin(phase)], 0)
    inverse = forward.T[block:] * (2.0 / period)
    return forward.astype(jnp.bfloat16), inverse.astype(jnp.bfloat16)


def layer(
    grid,
    blocks,
    chunks,
    feat_hbm,
    vw_hbm,
    gw_hbm,
    ker_hbm,
    skip_hbm,
    fwd_hbm,
    inv_hbm,
    out,
    feat,
    wgt,
    ktmp,
    skip,
    fwd,
    inv,
    kg,
    vsend,
    vrecv,
    gsend,
    grecv,
    vown,
    gown,
    xs,
    es,
    kh,
    ys,
    conv,
    relay,
    in_sem,
    feat_sem,
    v_ssem,
    v_rsem,
    g_ssem,
    g_rsem,
    h_ssem,
    h_rsem,
    a_sem,
    z_ssem,
    z_rsem,
    x_ssem,
    x_rsem,
    c_sem,
    s_sem,
    r_sem,
    q_sem,
    d_sem,
):
    n_yh, n_z, n_x, n_core = grid
    n_seq = n_yh * n_z * n_x * n_core
    rows = feat.shape[0]
    size = rows // chunks
    block = rows // blocks
    channels = vown.shape[1]
    seqs = n_seq // blocks

    me = lax.axis_index("seq")
    side = lax.axis_index("ch")
    core = me % n_core
    x = me // n_core % n_x
    z = me // (n_core * n_x) % n_z
    yh = me // (n_core * n_x * n_z)

    def seq_of(yh, z, x, core):
        return ((yh * n_z + z) * n_x + x) * n_core + core

    other = pl.ds(pl.multiple_of((1 - side) * channels, 128), channels)
    own = pl.ds(pl.multiple_of(side * channels, 128), channels)

    def feat_copy(i):
        part = pl.ds(pl.multiple_of(i * size, size), size)
        return pltpu.make_async_copy(feat_hbm.at[part], feat.at[part], feat_sem.at[i])

    weight_copies = [
        pltpu.make_async_copy(hbm.at[:, cols], wgt.at[j], in_sem.at[j])
        for j, (hbm, cols) in enumerate(
            ((vw_hbm, other), (vw_hbm, own), (gw_hbm, other), (gw_hbm, own))
        )
    ]
    small_copies = [
        pltpu.make_async_copy(hbm, ref, in_sem.at[4 + j])
        for j, (hbm, ref) in enumerate(
            (
                (ker_hbm, ktmp),
                (fwd_hbm, fwd),
                (inv_hbm, inv),
                (skip_hbm, skip),
            )
        )
    ]
    small_copies[0].start()
    feat_copy(0).start()
    weight_copies[0].start()
    for i in range(1, chunks):
        feat_copy(i).start()
    for copy in weight_copies[1:]:
        copy.start()
    for copy in small_copies[1:]:
        copy.start()

    partner = {"ch": 1 - side}
    following = {"seq": (me + 1) % n_seq}
    preceding = {"seq": (me + n_seq - 1) % n_seq}
    yh_partner = {"seq": seq_of(1 - yh, z, x, core)}
    core_partner = {"seq": seq_of(yh, z, x, 1 - core)}
    z_to = {d: {"seq": seq_of(yh, (z + d) % n_z, x, core)} for d in range(1, n_z)}
    x_to = {d: {"seq": seq_of(yh, z, (x + d) % n_x, core)} for d in range(1, n_x)}
    source, target = n_seq // 2 - 1, n_seq // 2
    at_end = (x == n_x - 1) & (core == n_core - 1)
    is_source = me == source
    is_first = at_end & (yh == 0) & (z < n_z - 1)
    at_seam = at_end & (yh == 0)
    is_second = at_end & (yh == 1)
    piece_rows = rows // n_z
    sends_halo = (me < n_seq - 1) & (me != source)
    gets_halo = (me > 0) & (me != target)

    late = n_z // 2
    others = [(z + d) % n_z for d in range(1, n_z)]
    z_devices = [{"seq": seq_of(yh, other, x, core)} for other in others]
    is_later = [(z < late) & (other > z) for other in others]
    is_earlier = [(other < late) & (other < z) for other in others]
    is_level = [(z >= late) & (other >= late) for other in others]
    leads = (core == n_core - 1) & sends_halo
    led = (core == 0) & gets_halo
    barrier = pltpu.get_barrier_semaphore()

    def signal(device):
        pl.semaphore_signal(barrier, inc=1, device_id=device, device_id_type=MESH)

    def signal_if(condition, device):
        @pl.when(condition)
        def _():
            signal(device)

    level = [partner, core_partner, yh_partner] + list(x_to.values())
    level_count = len(level)
    for device in level:
        signal(device)
    for device, condition in zip(z_devices, is_level):
        signal_if(condition, device)
    signal_if(led, preceding)

    @pl.when(me == target)
    def _():
        for j in range(n_z):
            signal({"seq": seq_of(1, j, n_x - 1, n_core - 1)})

    def count(*conditions):
        return sum(condition.astype(jnp.int32) for condition in conditions)

    def enter():
        pl.semaphore_wait(
            barrier,
            level_count
            + jnp.where(z < late, z, n_z - 1)
            + count(leads, is_second),
        )
        for device, later, earlier in zip(z_devices, is_later, is_earlier):
            signal_if(later | earlier, device)

    def hear_answers():
        pl.semaphore_wait(barrier, n_z - 1 - z)

    def remote(src, dst, ssem, rsem, device):
        return pltpu.make_async_remote_copy(
            src_ref=src,
            dst_ref=dst,
            send_sem=ssem,
            recv_sem=rsem,
            device_id=device,
            device_id_type=MESH,
        )

    def part(i):
        return pl.ds(pl.multiple_of(i * size, size), size)

    def v_copy(i):
        return remote(vsend.at[part(i)], vrecv.at[part(i)], v_ssem.at[i], v_rsem.at[i], partner)

    def g_copy(i):
        return remote(gsend.at[part(i)], grecv.at[part(i)], g_ssem.at[i], g_rsem.at[i], partner)

    def current(i):
        return pl.ds(pl.multiple_of(rows + i * size, size), size)

    def h_copy(i):
        return remote(xs.at[current(i)], xs.at[part(i)], h_ssem.at[i], h_rsem.at[i], following)

    def piece(j, start):
        return pl.ds(pl.multiple_of(start + j * piece_rows, piece_rows), piece_rows)

    def seam_first(j):
        device = {"seq": seq_of(0, j, n_x - 1, n_core - 1)}
        return remote(xs.at[piece(j, rows)], relay, s_sem.at[j], r_sem.at[0], device)

    def seam_last():
        return remote(xs.at[piece(n_z - 1, rows)], relay, r_sem.at[1], q_sem.at[0], yh_partner)

    def seam_second():
        return remote(relay, relay, r_sem.at[1], q_sem.at[0], yh_partner)

    def seam_third(j):
        return remote(relay, xs.at[piece(j, 0)], q_sem.at[1], d_sem.at[j], {"seq": target})

    def a_copy(sender):
        slot = kg.at[core, x, z, sender]
        return remote(slot, slot, a_sem.at[0], a_sem.at[1], yh_partner)

    def z_copy(d, sender):
        slot = kg.at[core, x, sender]
        return remote(slot, slot, z_ssem.at[d], z_rsem.at[d], z_to[d])

    def x_copy(d, sender):
        slot = kg.at[core, sender]
        return remote(slot, slot, x_ssem.at[d], x_rsem.at[d], x_to[d])

    def c_copy(sender):
        slot = kg.at[sender]
        return remote(slot, slot, c_sem.at[0], c_sem.at[1], core_partner)

    small_copies[0].wait()
    taps = ktmp[...].astype(jnp.float32)
    half = channels // 2
    kg[core, x, z, yh] = jnp.concatenate([taps[:, :half], taps[:, half:]], 0).astype(kg.dtype)

    weight_copies[0].wait()

    @pl.loop(0, chunks)
    def _(i):
        feat_copy(i).wait()
        total = jnp.dot(feat[part(i)], wgt[0], preferred_element_type=jnp.float32)
        vsend[part(i)] = total.astype(vsend.dtype)

        @pl.when(i == 0)
        def _():
            enter()
            a_copy(yh).start()

        v_copy(i).start()

    a_copy(1 - yh).wait_recv()

    @pl.when(z >= late)
    def _():
        for d in range(1, n_z):
            z_copy(d, z).start()

    weight_copies[1].wait()

    @pl.loop(0, chunks)
    def _(i):
        vown[part(i)] = jnp.dot(feat[part(i)], wgt[1], preferred_element_type=jnp.float32)

    weight_copies[2].wait()

    @pl.loop(0, chunks)
    def _(i):
        total = jnp.dot(feat[part(i)], wgt[2], preferred_element_type=jnp.float32)
        gsend[part(i)] = total.astype(gsend.dtype)

    @pl.when(z < late)
    def _():
        hear_answers()
        for d in range(1, n_z):
            z_copy(d, z).start()

    weight_copies[3].wait()

    @pl.loop(0, chunks)
    def _(i):
        gown[part(i)] = jnp.dot(feat[part(i)], wgt[3], preferred_element_type=jnp.float32)

    for d in range(1, n_z):
        z_copy(d, (z + n_z - d) % n_z).wait_recv()
    for d in range(1, n_x):
        x_copy(d, x).start()

    def arrived(i):
        v_copy(i).wait_recv()
        total = vown[part(i)] + vrecv[part(i)].astype(jnp.float32)
        xs[current(i)] = total.astype(xs.dtype)

        @pl.when(sends_halo)
        def _():
            h_copy(i).start()

        @pl.when(is_source)
        def _():
            for j in range(i * n_z // chunks, (i + 1) * n_z // chunks):
                if j < n_z - 1:
                    seam_first(j).start()
                else:
                    seam_last().start()

    for i in range(chunks):
        arrived(i)
        if i == chunks - 2:

            @pl.when(jnp.logical_not(at_seam))
            def _():
                g_copy(0).start()

    @pl.when(is_first)
    def _():
        seam_first(z).wait_recv()
        seam_second().start()

    @pl.when(at_seam)
    def _():
        g_copy(0).start()

    for i in range(1, chunks):
        g_copy(i).start()

    def forward(m):
        pair = xs[pl.ds(pl.multiple_of(m * block, block), 2 * block)]
        es[m] = jnp.dot(fwd[...], pair, preferred_element_type=jnp.float32)

    def products(first, last):
        more = first == 0

        @pl.loop(0, block // 8)
        def _(r):
            real = pl.ds(pl.multiple_of(r * 8, 8), 8)
            imag = pl.ds(pl.multiple_of(block + r * 8, 8), 8)
            for part_of in range(2):
                lanes = pl.ds(part_of * half, half)
                k_real = [kh[p, real, lanes] for p in range(blocks)]
                k_imag = [kh[p, imag, lanes] for p in range(blocks)]
                sum_real = [ys[a, real, lanes] if more and a else None for a in range(blocks)]
                sum_imag = [ys[a, imag, lanes] if more and a else None for a in range(blocks)]
                for m in range(first, last):
                    e_real, e_imag = es[m, real, lanes], es[m, imag, lanes]
                    for a in range(blocks):
                        p = blocks - 1 + a - m
                        if not 0 <= p < blocks:
                            continue
                        new_real = e_real * k_real[p] - e_imag * k_imag[p]
                        new_imag = e_imag * k_real[p] + e_real * k_imag[p]
                        if sum_real[a] is None:
                            sum_real[a], sum_imag[a] = new_real, new_imag
                        else:
                            sum_real[a] = sum_real[a] + new_real
                            sum_imag[a] = sum_imag[a] + new_imag
                for a in range(blocks):
                    if sum_real[a] is not None:
                        ys[a, real, lanes] = sum_real[a]
                        ys[a, imag, lanes] = sum_imag[a]

    def transform_taps():
        c_copy(1 - core).wait_recv()
        for p in range(blocks):
            pieces = []
            for seq in range(p * seqs, (p + 1) * seqs):
                at_core, at_x = seq % n_core, seq // n_core % n_x
                at_z, at_yh = seq // (n_core * n_x) % n_z, seq // (n_core * n_x * n_z)
                taps = kg[at_core, at_x, at_z, at_yh].astype(jnp.float32)
                pieces.append(jnp.concatenate([taps[:8], taps[8:]], 1))
            taps = jnp.concatenate(pieces, 0).astype(jnp.bfloat16)
            kh[p] = jnp.dot(fwd[:, :block], taps, preferred_element_type=jnp.float32)

    def transform_halo():
        done = 0
        for i in range(chunks):

            @pl.when(gets_halo)
            def _():
                h_copy(i).wait_recv()

            @pl.when(me == target)
            def _():
                for j in range(i * n_z // chunks, (i + 1) * n_z // chunks):
                    seam_third(j).wait_recv()

            ready = blocks if i == chunks - 1 else (i + 1) * blocks // chunks - 1
            pl.loop(done, ready)(forward)
            done = ready

    for copy in small_copies[1:]:
        copy.wait()
    pl.loop(blocks, 2 * blocks - 1)(forward)
    for d in range(1, n_x):
        x_copy(d, (x + n_x - d) % n_x).wait_recv()
    c_copy(core).start()

    @pl.when(me == 0)
    def _():
        xs[pl.ds(0, rows)] = jnp.zeros((rows, channels), xs.dtype)

    @pl.when(is_second)
    def _():
        seam_second().wait_recv()
        seam_third(z).start()

    taps_last = (z < late) & (me != target)

    @pl.when(taps_last)
    def _():
        transform_halo()
        transform_taps()
        products(blocks, 2 * blocks - 1)

    @pl.when(jnp.logical_not(taps_last))
    def _():
        transform_taps()
        products(blocks, 2 * blocks - 1)
        transform_halo()

    products(0, blocks)

    gain = skip[...]

    @pl.loop(0, blocks)
    def _(a):
        spectrum = ys[a].astype(jnp.bfloat16)
        back = jnp.dot(inv[...], spectrum, preferred_element_type=jnp.float32)
        direct = xs[pl.ds(pl.multiple_of(rows + a * block, block), block)].astype(jnp.float32)
        conv[pl.ds(pl.multiple_of(a * block, block), block)] = back + gain * direct

    @pl.loop(0, chunks)
    def _(i):
        g_copy(i).wait_recv()
        gate = gown[part(i)] + grecv[part(i)].astype(jnp.float32)
        out[part(i)] = (conv[part(i)] * (gate / (1.0 + jnp.exp(-gate)))).astype(out.dtype)

    for i in range(chunks):
        v_copy(i).wait_send()
        g_copy(i).wait_send()

    @pl.when(sends_halo)
    def _():
        for i in range(chunks):
            h_copy(i).wait_send()

    a_copy(yh).wait_send()
    for d in range(1, n_z):
        z_copy(d, z).wait_send()
    for d in range(1, n_x):
        x_copy(d, x).wait_send()
    c_copy(core).wait_send()

    @pl.when(is_source)
    def _():
        for j in range(n_z - 1):
            seam_first(j).wait_send()
        seam_last().wait_send()

    @pl.when(is_first)
    def _():
        seam_second().wait_send()

    @pl.when(is_second)
    def _():
        seam_third(z).wait_send()


def solution(mesh, grid=GRID, blocks=BLOCKS, chunks=CHUNKS):
    def on_device(features, value_weight, gate_weight, kernel, skip_gain):
        rows, depth = features.shape
        tap_rows, channels = kernel.shape
        block = rows // blocks
        fwd, inv = tables(block)
        f32, bf16 = jnp.float32, jnp.bfloat16
        dma = pltpu.SemaphoreType.DMA
        n_yh, n_z, n_x, n_core = grid
        return pl.pallas_call(
            functools.partial(layer, grid, blocks, chunks),
            out_shape=pltpu.VMEM((rows, channels), bf16),
            in_specs=[pl.BlockSpec(memory_space=pl.ANY)] * 7,
            out_specs=pl.BlockSpec(memory_space=pltpu.VMEM),
            scratch_shapes=[
                pltpu.VMEM((rows, depth), bf16),
                pltpu.VMEM((4, depth, channels), bf16),
                pltpu.VMEM((tap_rows, channels), bf16),
                pltpu.VMEM((1, channels), f32),
                pltpu.VMEM(fwd.shape, bf16),
                pltpu.VMEM(inv.shape, bf16),
                pltpu.VMEM((n_core, n_x, n_z, n_yh, 2 * tap_rows, channels // 2), bf16),
                pltpu.VMEM((rows, channels), WIRE),
                pltpu.VMEM((rows, channels), WIRE),
                pltpu.VMEM((rows, channels), WIRE),
                pltpu.VMEM((rows, channels), WIRE),
                pltpu.VMEM((rows, channels), f32),
                pltpu.VMEM((rows, channels), f32),
                pltpu.VMEM((2 * rows, channels), bf16),
                pltpu.VMEM((2 * blocks - 1, 2 * block, channels), f32),
                pltpu.VMEM((blocks, 2 * block, channels), f32),
                pltpu.VMEM((blocks, 2 * block, channels), f32),
                pltpu.VMEM((rows, channels), f32),
                pltpu.VMEM((rows // n_z, channels), bf16),
                dma((9,)),
                dma((chunks,)),
                dma((chunks,)),
                dma((chunks,)),
                dma((chunks,)),
                dma((chunks,)),
                dma((chunks,)),
                dma((chunks,)),
                dma((2,)),
                dma((n_z,)),
                dma((n_z,)),
                dma((n_x,)),
                dma((n_x,)),
                dma((2,)),
                dma((n_z,)),
                dma((2,)),
                dma((2,)),
                dma((n_z,)),
            ],
            compiler_params=pltpu.CompilerParams(
                collective_id=0, has_side_effects=True, vmem_limit_bytes=56 * 2**20
            ),
            cost_estimate=pl.CostEstimate(
                flops=8 * rows * depth * channels,
                bytes_accessed=2 * (rows * depth + 4 * depth * channels + rows * channels),
                transcendentals=rows * channels,
            ),
        )(
            features,
            value_weight,
            gate_weight,
            kernel,
            skip_gain.reshape(1, channels),
            jnp.asarray(fwd),
            jnp.asarray(inv),
        )

    return jax.shard_map(
        on_device,
        mesh=mesh,
        in_specs=(P("seq", "ch"), P("ch", None), P("ch", None), P("seq", "ch"), P("ch")),
        out_specs=P("seq", "ch"),
        check_vma=False,
    )
```

```python
import functools
import math

import jax
import jax.numpy as jnp
import numpy as np
from jax import lax
from jax.experimental import pallas as pl
from jax.experimental.pallas import tpu as pltpu
from jax.sharding import PartitionSpec as P

MESH = pl.DeviceIdType.MESH
WIRE = jnp.bfloat16
GRID = (2, 8, 4, 2)
BLOCKS = 8
CHUNKS = 4


def tables(block):
    period = 2 * block
    freq = np.arange(block)[:, None] + 0.5
    place = np.arange(period)[None, :]
    phase = 2.0 * math.pi * freq * place / period
    forward = np.concatenate([np.cos(phase), np.sin(phase)], 0)
    inverse = forward.T[block:] * (2.0 / period)
    return forward.astype(jnp.bfloat16), inverse.astype(jnp.bfloat16)


def layer(
    grid,
    blocks,
    chunks,
    feat_hbm,
    vw_hbm,
    gw_hbm,
    ker_hbm,
    skip_hbm,
    fwd_hbm,
    inv_hbm,
    out,
    feat,
    wgt,
    ktmp,
    skip,
    fwd,
    inv,
    kg,
    vsend,
    vrecv,
    gsend,
    grecv,
    vown,
    gown,
    xs,
    es,
    kh,
    ys,
    conv,
    relay,
    in_sem,
    feat_sem,
    v_ssem,
    v_rsem,
    g_ssem,
    g_rsem,
    h_ssem,
    h_rsem,
    a_sem,
    z_ssem,
    z_rsem,
    x_ssem,
    x_rsem,
    c_sem,
    s_sem,
    r_sem,
    d_sem,
):
    n_yh, n_z, n_x, n_core = grid
    n_seq = n_yh * n_z * n_x * n_core
    rows = feat.shape[0]
    size = rows // chunks
    block = rows // blocks
    channels = vown.shape[1]
    seqs = n_seq // blocks

    me = lax.axis_index("seq")
    side = lax.axis_index("ch")
    core = me % n_core
    x = me // n_core % n_x
    z = me // (n_core * n_x) % n_z
    yh = me // (n_core * n_x * n_z)

    def seq_of(yh, z, x, core):
        return ((yh * n_z + z) * n_x + x) * n_core + core

    other = pl.ds(pl.multiple_of((1 - side) * channels, 128), channels)
    own = pl.ds(pl.multiple_of(side * channels, 128), channels)

    def feat_copy(i):
        part = pl.ds(pl.multiple_of(i * size, size), size)
        return pltpu.make_async_copy(feat_hbm.at[part], feat.at[part], feat_sem.at[i])

    weight_copies = [
        pltpu.make_async_copy(hbm.at[:, cols], wgt.at[j], in_sem.at[j])
        for j, (hbm, cols) in enumerate(
            ((vw_hbm, other), (vw_hbm, own), (gw_hbm, other), (gw_hbm, own))
        )
    ]
    small_copies = [
        pltpu.make_async_copy(hbm, ref, in_sem.at[4 + j])
        for j, (hbm, ref) in enumerate(
            (
                (ker_hbm, ktmp),
                (fwd_hbm, fwd),
                (inv_hbm, inv),
                (skip_hbm, skip),
            )
        )
    ]
    small_copies[0].start()
    feat_copy(0).start()
    weight_copies[0].start()
    for i in range(1, chunks):
        feat_copy(i).start()
    for copy in weight_copies[1:]:
        copy.start()
    for copy in small_copies[1:]:
        copy.start()

    partner = {"ch": 1 - side}
    following = {"seq": (me + 1) % n_seq}
    preceding = {"seq": (me + n_seq - 1) % n_seq}
    yh_partner = {"seq": seq_of(1 - yh, z, x, core)}
    core_partner = {"seq": seq_of(yh, z, x, 1 - core)}
    z_to = {d: {"seq": seq_of(yh, (z + d) % n_z, x, core)} for d in range(1, n_z)}
    x_to = {d: {"seq": seq_of(yh, z, (x + d) % n_x, core)} for d in range(1, n_x)}
    source, target = n_seq // 2 - 1, n_seq // 2
    at_end = (x == n_x - 1) & (core == n_core - 1)
    is_source = me == source
    relays = at_end & (yh == 1)
    piece_rows = rows // n_z
    sends_halo = (me < n_seq - 1) & (me != source)
    gets_halo = (me > 0) & (me != target)

    late = n_z // 2
    others = [(z + d) % n_z for d in range(1, n_z)]
    z_devices = [{"seq": seq_of(yh, other, x, core)} for other in others]
    is_later = [(z < late) & (other > z) for other in others]
    is_earlier = [(other < late) & (other < z) for other in others]
    is_level = [(z >= late) & (other >= late) for other in others]
    leads = (core == n_core - 1) & sends_halo
    led = (core == 0) & gets_halo
    barrier = pltpu.get_barrier_semaphore()

    def signal(device):
        pl.semaphore_signal(barrier, inc=1, device_id=device, device_id_type=MESH)

    def signal_if(condition, device):
        @pl.when(condition)
        def _():
            signal(device)

    level = [partner, core_partner, yh_partner] + list(x_to.values())
    level_count = len(level)
    for device in level:
        signal(device)
    for device, condition in zip(z_devices, is_level):
        signal_if(condition, device)
    signal_if(led, preceding)

    @pl.when(me == target)
    def _():
        for j in range(n_z):
            signal({"seq": seq_of(1, j, n_x - 1, n_core - 1)})

    signal_if(relays, {"seq": source})

    def count(*conditions):
        return sum(condition.astype(jnp.int32) for condition in conditions)

    def enter():
        pl.semaphore_wait(
            barrier,
            level_count
            + jnp.where(z < late, z, n_z - 1)
            + count(leads, relays)
            + jnp.where(is_source, n_z, 0),
        )
        for device, later, earlier in zip(z_devices, is_later, is_earlier):
            signal_if(later | earlier, device)

    def hear_answers():
        pl.semaphore_wait(barrier, n_z - 1 - z)

    def remote(src, dst, ssem, rsem, device):
        return pltpu.make_async_remote_copy(
            src_ref=src,
            dst_ref=dst,
            send_sem=ssem,
            recv_sem=rsem,
            device_id=device,
            device_id_type=MESH,
        )

    def part(i):
        return pl.ds(pl.multiple_of(i * size, size), size)

    def v_copy(i):
        return remote(vsend.at[part(i)], vrecv.at[part(i)], v_ssem.at[i], v_rsem.at[i], partner)

    def g_copy(i):
        return remote(gsend.at[part(i)], grecv.at[part(i)], g_ssem.at[i], g_rsem.at[i], partner)

    def current(i):
        return pl.ds(pl.multiple_of(rows + i * size, size), size)

    def h_copy(i):
        return remote(xs.at[current(i)], xs.at[part(i)], h_ssem.at[i], h_rsem.at[i], following)

    def piece(j, start):
        return pl.ds(pl.multiple_of(start + j * piece_rows, piece_rows), piece_rows)

    def seam_first(j):
        device = {"seq": seq_of(1, j, n_x - 1, n_core - 1)}
        return remote(xs.at[piece(j, rows)], relay, s_sem.at[j], r_sem.at[0], device)

    def seam_second(j):
        return remote(relay, xs.at[piece(j, 0)], r_sem.at[1], d_sem.at[j], {"seq": target})

    def a_copy(sender):
        slot = kg.at[core, x, z, sender]
        return remote(slot, slot, a_sem.at[0], a_sem.at[1], yh_partner)

    def z_copy(d, sender):
        slot = kg.at[core, x, sender]
        return remote(slot, slot, z_ssem.at[d], z_rsem.at[d], z_to[d])

    def x_copy(d, sender):
        slot = kg.at[core, sender]
        return remote(slot, slot, x_ssem.at[d], x_rsem.at[d], x_to[d])

    def c_copy(sender):
        slot = kg.at[sender]
        return remote(slot, slot, c_sem.at[0], c_sem.at[1], core_partner)

    small_copies[0].wait()
    taps = ktmp[...].astype(jnp.float32)
    half = channels // 2
    kg[core, x, z, yh] = jnp.concatenate([taps[:, :half], taps[:, half:]], 0).astype(kg.dtype)

    weight_copies[0].wait()

    @pl.loop(0, chunks)
    def _(i):
        feat_copy(i).wait()
        total = jnp.dot(feat[part(i)], wgt[0], preferred_element_type=jnp.float32)
        vsend[part(i)] = total.astype(vsend.dtype)

        @pl.when(i == 0)
        def _():
            enter()
            a_copy(yh).start()

        v_copy(i).start()

    def arrived(i):
        v_copy(i).wait_recv()
        total = vown[part(i)] + vrecv[part(i)].astype(jnp.float32)
        xs[current(i)] = total.astype(xs.dtype)

        @pl.when(sends_halo)
        def _():
            h_copy(i).start()

        @pl.when(is_source)
        def _():
            for j in range(i * n_z // chunks, (i + 1) * n_z // chunks):
                seam_first(j).start()

    a_copy(1 - yh).wait_recv()

    @pl.when(z >= late)
    def _():
        for d in range(1, n_z):
            z_copy(d, z).start()

    weight_copies[1].wait()

    @pl.loop(0, chunks)
    def _(i):
        vown[part(i)] = jnp.dot(feat[part(i)], wgt[1], preferred_element_type=jnp.float32)

    early = chunks - 2
    for i in range(early // 2):
        arrived(i)

    weight_copies[2].wait()

    @pl.loop(0, chunks)
    def _(i):
        total = jnp.dot(feat[part(i)], wgt[2], preferred_element_type=jnp.float32)
        gsend[part(i)] = total.astype(gsend.dtype)

    for i in range(early // 2, early):
        arrived(i)

    @pl.when(z < late)
    def _():
        hear_answers()
        for d in range(1, n_z):
            z_copy(d, z).start()

    weight_copies[3].wait()

    @pl.loop(0, chunks)
    def _(i):
        gown[part(i)] = jnp.dot(feat[part(i)], wgt[3], preferred_element_type=jnp.float32)

    arrived(chunks - 2)
    g_copy(0).start()

    for d in range(1, n_z):
        z_copy(d, (z + n_z - d) % n_z).wait_recv()
    for d in range(1, n_x):
        x_copy(d, x).start()

    arrived(chunks - 1)

    for i in range(1, chunks):
        g_copy(i).start()

    @pl.when(relays)
    def _():
        seam_first(z).wait_recv()
        seam_second(z).start()

    def forward(m):
        pair = xs[pl.ds(pl.multiple_of(m * block, block), 2 * block)]
        es[m] = jnp.dot(fwd[...], pair, preferred_element_type=jnp.float32)

    def products(first, last):
        more = first == 0

        @pl.loop(0, block // 8)
        def _(r):
            real = pl.ds(pl.multiple_of(r * 8, 8), 8)
            imag = pl.ds(pl.multiple_of(block + r * 8, 8), 8)
            for part_of in range(2):
                lanes = pl.ds(part_of * half, half)
                k_real = [kh[p, real, lanes] for p in range(blocks)]
                k_imag = [kh[p, imag, lanes] for p in range(blocks)]
                sum_real = [ys[a, real, lanes] if more and a else None for a in range(blocks)]
                sum_imag = [ys[a, imag, lanes] if more and a else None for a in range(blocks)]
                for m in range(first, last):
                    e_real, e_imag = es[m, real, lanes], es[m, imag, lanes]
                    for a in range(blocks):
                        p = blocks - 1 + a - m
                        if not 0 <= p < blocks:
                            continue
                        new_real = e_real * k_real[p] - e_imag * k_imag[p]
                        new_imag = e_imag * k_real[p] + e_real * k_imag[p]
                        if sum_real[a] is None:
                            sum_real[a], sum_imag[a] = new_real, new_imag
                        else:
                            sum_real[a] = sum_real[a] + new_real
                            sum_imag[a] = sum_imag[a] + new_imag
                for a in range(blocks):
                    if sum_real[a] is not None:
                        ys[a, real, lanes] = sum_real[a]
                        ys[a, imag, lanes] = sum_imag[a]

    def transform_taps():
        c_copy(1 - core).wait_recv()
        for p in range(blocks):
            pieces = []
            for seq in range(p * seqs, (p + 1) * seqs):
                at_core, at_x = seq % n_core, seq // n_core % n_x
                at_z, at_yh = seq // (n_core * n_x) % n_z, seq // (n_core * n_x * n_z)
                taps = kg[at_core, at_x, at_z, at_yh].astype(jnp.float32)
                pieces.append(jnp.concatenate([taps[:8], taps[8:]], 1))
            taps = jnp.concatenate(pieces, 0).astype(jnp.bfloat16)
            kh[p] = jnp.dot(fwd[:, :block], taps, preferred_element_type=jnp.float32)

    def transform_halo():
        done = 0
        for i in range(chunks):

            @pl.when(gets_halo)
            def _():
                h_copy(i).wait_recv()

            @pl.when(me == target)
            def _():
                for j in range(i * n_z // chunks, (i + 1) * n_z // chunks):
                    seam_second(j).wait_recv()

            ready = blocks if i == chunks - 1 else (i + 1) * blocks // chunks - 1
            pl.loop(done, ready)(forward)
            done = ready

    for copy in small_copies[1:]:
        copy.wait()
    pl.loop(blocks, 2 * blocks - 1)(forward)

    for d in range(1, n_x):
        x_copy(d, (x + n_x - d) % n_x).wait_recv()
    c_copy(core).start()

    @pl.when(me == 0)
    def _():
        xs[pl.ds(0, rows)] = jnp.zeros((rows, channels), xs.dtype)

    taps_last = (z < late) & (me != target)

    @pl.when(taps_last)
    def _():
        transform_halo()
        transform_taps()
        products(blocks, 2 * blocks - 1)

    @pl.when(jnp.logical_not(taps_last))
    def _():
        transform_taps()
        products(blocks, 2 * blocks - 1)
        transform_halo()

    products(0, blocks)

    gain = skip[...]

    @pl.loop(0, blocks)
    def _(a):
        spectrum = ys[a].astype(jnp.bfloat16)
        back = jnp.dot(inv[...], spectrum, preferred_element_type=jnp.float32)
        direct = xs[pl.ds(pl.multiple_of(rows + a * block, block), block)].astype(jnp.float32)
        conv[pl.ds(pl.multiple_of(a * block, block), block)] = back + gain * direct

    @pl.loop(0, chunks)
    def _(i):
        g_copy(i).wait_recv()
        gate = gown[part(i)] + grecv[part(i)].astype(jnp.float32)
        out[part(i)] = (conv[part(i)] * (gate / (1.0 + jnp.exp(-gate)))).astype(out.dtype)

    for i in range(chunks):
        v_copy(i).wait_send()
        g_copy(i).wait_send()

    @pl.when(sends_halo)
    def _():
        for i in range(chunks):
            h_copy(i).wait_send()

    a_copy(yh).wait_send()
    for d in range(1, n_z):
        z_copy(d, z).wait_send()
    for d in range(1, n_x):
        x_copy(d, x).wait_send()
    c_copy(core).wait_send()

    @pl.when(is_source)
    def _():
        for j in range(n_z):
            seam_first(j).wait_send()

    @pl.when(relays)
    def _():
        seam_second(z).wait_send()


def solution(mesh, grid=GRID, blocks=BLOCKS, chunks=CHUNKS):
    def on_device(features, value_weight, gate_weight, kernel, skip_gain):
        rows, depth = features.shape
        tap_rows, channels = kernel.shape
        block = rows // blocks
        fwd, inv = tables(block)
        f32, bf16 = jnp.float32, jnp.bfloat16
        dma = pltpu.SemaphoreType.DMA
        n_yh, n_z, n_x, n_core = grid
        return pl.pallas_call(
            functools.partial(layer, grid, blocks, chunks),
            out_shape=pltpu.VMEM((rows, channels), bf16),
            in_specs=[pl.BlockSpec(memory_space=pl.ANY)] * 7,
            out_specs=pl.BlockSpec(memory_space=pltpu.VMEM),
            scratch_shapes=[
                pltpu.VMEM((rows, depth), bf16),
                pltpu.VMEM((4, depth, channels), bf16),
                pltpu.VMEM((tap_rows, channels), bf16),
                pltpu.VMEM((1, channels), f32),
                pltpu.VMEM(fwd.shape, bf16),
                pltpu.VMEM(inv.shape, bf16),
                pltpu.VMEM((n_core, n_x, n_z, n_yh, 2 * tap_rows, channels // 2), bf16),
                pltpu.VMEM((rows, channels), WIRE),
                pltpu.VMEM((rows, channels), WIRE),
                pltpu.VMEM((rows, channels), WIRE),
                pltpu.VMEM((rows, channels), WIRE),
                pltpu.VMEM((rows, channels), f32),
                pltpu.VMEM((rows, channels), f32),
                pltpu.VMEM((2 * rows, channels), bf16),
                pltpu.VMEM((2 * blocks - 1, 2 * block, channels), f32),
                pltpu.VMEM((blocks, 2 * block, channels), f32),
                pltpu.VMEM((blocks, 2 * block, channels), f32),
                pltpu.VMEM((rows, channels), f32),
                pltpu.VMEM((rows // n_z, channels), bf16),
                dma((9,)),
                dma((chunks,)),
                dma((chunks,)),
                dma((chunks,)),
                dma((chunks,)),
                dma((chunks,)),
                dma((chunks,)),
                dma((chunks,)),
                dma((2,)),
                dma((n_z,)),
                dma((n_z,)),
                dma((n_x,)),
                dma((n_x,)),
                dma((2,)),
                dma((n_z,)),
                dma((2,)),
                dma((n_z,)),
            ],
            compiler_params=pltpu.CompilerParams(
                collective_id=0, has_side_effects=True, vmem_limit_bytes=56 * 2**20
            ),
            cost_estimate=pl.CostEstimate(
                flops=8 * rows * depth * channels,
                bytes_accessed=2 * (rows * depth + 4 * depth * channels + rows * channels),
                transcendentals=rows * channels,
            ),
        )(
            features,
            value_weight,
            gate_weight,
            kernel,
            skip_gain.reshape(1, channels),
            jnp.asarray(fwd),
            jnp.asarray(inv),
        )

    return jax.shard_map(
        on_device,
        mesh=mesh,
        in_specs=(P("seq", "ch"), P("ch", None), P("ch", None), P("seq", "ch"), P("ch")),
        out_specs=P("seq", "ch"),
        check_vma=False,
    )
```

```python
import functools
import math

import jax
import jax.numpy as jnp
import numpy as np
from jax import lax
from jax.experimental import pallas as pl
from jax.experimental.pallas import tpu as pltpu
from jax.sharding import PartitionSpec as P

MESH = pl.DeviceIdType.MESH
WIRE = jnp.bfloat16
GRID = (2, 8, 4, 2)
BLOCKS = 8
CHUNKS = 4


def tables(block):
    period = 2 * block
    freq = np.arange(block)[:, None] + 0.5
    place = np.arange(period)[None, :]
    phase = 2.0 * math.pi * freq * place / period
    forward = np.concatenate([np.cos(phase), np.sin(phase)], 0)
    inverse = forward.T[block:] * (2.0 / period)
    return forward.astype(jnp.bfloat16), inverse.astype(jnp.bfloat16)


def layer(
    grid,
    blocks,
    chunks,
    feat_hbm,
    vw_hbm,
    gw_hbm,
    ker_hbm,
    skip_hbm,
    fwd_hbm,
    inv_hbm,
    out,
    feat,
    wgt,
    ktmp,
    skip,
    fwd,
    inv,
    kg,
    vsend,
    vrecv,
    gsend,
    grecv,
    vown,
    gown,
    xs,
    es,
    kh,
    ys,
    conv,
    relay,
    in_sem,
    feat_sem,
    v_ssem,
    v_rsem,
    g_ssem,
    g_rsem,
    h_ssem,
    h_rsem,
    a_sem,
    z_ssem,
    z_rsem,
    x_ssem,
    x_rsem,
    c_sem,
    s_sem,
    r_sem,
    d_sem,
):
    n_yh, n_z, n_x, n_core = grid
    n_seq = n_yh * n_z * n_x * n_core
    rows = feat.shape[0]
    size = rows // chunks
    block = rows // blocks
    channels = vown.shape[1]
    seqs = n_seq // blocks

    me = lax.axis_index("seq")
    side = lax.axis_index("ch")
    core = me % n_core
    x = me // n_core % n_x
    z = me // (n_core * n_x) % n_z
    yh = me // (n_core * n_x * n_z)

    def seq_of(yh, z, x, core):
        return ((yh * n_z + z) * n_x + x) * n_core + core

    other = pl.ds(pl.multiple_of((1 - side) * channels, 128), channels)
    own = pl.ds(pl.multiple_of(side * channels, 128), channels)

    def feat_copy(i):
        part = pl.ds(pl.multiple_of(i * size, size), size)
        return pltpu.make_async_copy(feat_hbm.at[part], feat.at[part], feat_sem.at[i])

    weight_copies = [
        pltpu.make_async_copy(hbm.at[:, cols], wgt.at[j], in_sem.at[j])
        for j, (hbm, cols) in enumerate(
            ((vw_hbm, other), (vw_hbm, own), (gw_hbm, other), (gw_hbm, own))
        )
    ]
    small_copies = [
        pltpu.make_async_copy(hbm, ref, in_sem.at[4 + j])
        for j, (hbm, ref) in enumerate(
            (
                (ker_hbm, ktmp),
                (fwd_hbm, fwd),
                (inv_hbm, inv),
                (skip_hbm, skip),
            )
        )
    ]
    small_copies[0].start()
    feat_copy(0).start()
    weight_copies[0].start()
    for i in range(1, chunks):
        feat_copy(i).start()
    for copy in weight_copies[1:]:
        copy.start()
    for copy in small_copies[1:]:
        copy.start()

    partner = {"ch": 1 - side}
    following = {"seq": (me + 1) % n_seq}
    preceding = {"seq": (me + n_seq - 1) % n_seq}
    yh_partner = {"seq": seq_of(1 - yh, z, x, core)}
    core_partner = {"seq": seq_of(yh, z, x, 1 - core)}
    z_to = {d: {"seq": seq_of(yh, (z + d) % n_z, x, core)} for d in range(1, n_z)}
    x_to = {d: {"seq": seq_of(yh, z, (x + d) % n_x, core)} for d in range(1, n_x)}
    source, target = n_seq // 2 - 1, n_seq // 2
    at_end = (x == n_x - 1) & (core == n_core - 1)
    is_source = me == source
    relays = at_end & (yh == 1)
    piece_rows = rows // n_z
    sends_halo = (me < n_seq - 1) & (me != source)
    gets_halo = (me > 0) & (me != target)

    late = n_z // 2
    others = [(z + d) % n_z for d in range(1, n_z)]
    z_devices = [{"seq": seq_of(yh, other, x, core)} for other in others]
    is_later = [(z < late) & (other > z) for other in others]
    is_earlier = [(other < late) & (other < z) for other in others]
    is_level = [(z >= late) & (other >= late) for other in others]
    leads = (core == n_core - 1) & sends_halo
    led = (core == 0) & gets_halo
    barrier = pltpu.get_barrier_semaphore()

    def signal(device):
        pl.semaphore_signal(barrier, inc=1, device_id=device, device_id_type=MESH)

    def signal_if(condition, device):
        @pl.when(condition)
        def _():
            signal(device)

    level = [partner, core_partner, yh_partner] + list(x_to.values())
    level_count = len(level)
    for device in level:
        signal(device)
    for device, condition in zip(z_devices, is_level):
        signal_if(condition, device)
    signal_if(led, preceding)

    @pl.when(me == target)
    def _():
        for j in range(n_z):
            signal({"seq": seq_of(1, j, n_x - 1, n_core - 1)})

    signal_if(relays, {"seq": source})

    def count(*conditions):
        return sum(condition.astype(jnp.int32) for condition in conditions)

    def enter():
        pl.semaphore_wait(
            barrier,
            level_count
            + jnp.where(z < late, z, n_z - 1)
            + count(leads, relays)
            + jnp.where(is_source, n_z, 0),
        )
        for device, later, earlier in zip(z_devices, is_later, is_earlier):
            signal_if(later | earlier, device)

    def hear_answers():
        pl.semaphore_wait(barrier, n_z - 1 - z)

    def remote(src, dst, ssem, rsem, device):
        return pltpu.make_async_remote_copy(
            src_ref=src,
            dst_ref=dst,
            send_sem=ssem,
            recv_sem=rsem,
            device_id=device,
            device_id_type=MESH,
        )

    def part(i):
        return pl.ds(pl.multiple_of(i * size, size), size)

    def v_copy(i):
        return remote(vsend.at[part(i)], vrecv.at[part(i)], v_ssem.at[i], v_rsem.at[i], partner)

    def g_copy(i):
        return remote(gsend.at[part(i)], grecv.at[part(i)], g_ssem.at[i], g_rsem.at[i], partner)

    def current(i):
        return pl.ds(pl.multiple_of(rows + i * size, size), size)

    def h_copy(i):
        return remote(xs.at[current(i)], xs.at[part(i)], h_ssem.at[i], h_rsem.at[i], following)

    def piece(j, start):
        return pl.ds(pl.multiple_of(start + j * piece_rows, piece_rows), piece_rows)

    def seam_first(j):
        device = {"seq": seq_of(1, n_z - 1 - j, n_x - 1, n_core - 1)}
        return remote(xs.at[piece(j, rows)], relay, s_sem.at[j], r_sem.at[0], device)

    def seam_second(j):
        return remote(relay, xs.at[piece(j, 0)], r_sem.at[1], d_sem.at[j], {"seq": target})

    def a_copy(sender):
        slot = kg.at[core, x, z, sender]
        return remote(slot, slot, a_sem.at[0], a_sem.at[1], yh_partner)

    def z_copy(d, sender):
        slot = kg.at[core, x, sender]
        return remote(slot, slot, z_ssem.at[d], z_rsem.at[d], z_to[d])

    def x_copy(d, sender):
        slot = kg.at[core, sender]
        return remote(slot, slot, x_ssem.at[d], x_rsem.at[d], x_to[d])

    def c_copy(sender):
        slot = kg.at[sender]
        return remote(slot, slot, c_sem.at[0], c_sem.at[1], core_partner)

    small_copies[0].wait()
    taps = ktmp[...].astype(jnp.float32)
    half = channels // 2
    kg[core, x, z, yh] = jnp.concatenate([taps[:, :half], taps[:, half:]], 0).astype(kg.dtype)

    weight_copies[0].wait()

    @pl.loop(0, chunks)
    def _(i):
        feat_copy(i).wait()
        total = jnp.dot(feat[part(i)], wgt[0], preferred_element_type=jnp.float32)
        vsend[part(i)] = total.astype(vsend.dtype)

        @pl.when(i == 0)
        def _():
            enter()
            a_copy(yh).start()

        v_copy(i).start()

    def arrived(i):
        v_copy(i).wait_recv()
        total = vown[part(i)] + vrecv[part(i)].astype(jnp.float32)
        xs[current(i)] = total.astype(xs.dtype)

        @pl.when(sends_halo)
        def _():
            h_copy(i).start()

        @pl.when(is_source)
        def _():
            for j in range(i * n_z // chunks, (i + 1) * n_z // chunks):
                seam_first(j).start()

    a_copy(1 - yh).wait_recv()

    @pl.when(z >= late)
    def _():
        for d in range(1, n_z):
            z_copy(d, z).start()

    weight_copies[1].wait()

    @pl.loop(0, chunks)
    def _(i):
        vown[part(i)] = jnp.dot(feat[part(i)], wgt[1], preferred_element_type=jnp.float32)

    early = chunks - 2
    for i in range(early // 2):
        arrived(i)

    weight_copies[2].wait()

    @pl.loop(0, chunks)
    def _(i):
        total = jnp.dot(feat[part(i)], wgt[2], preferred_element_type=jnp.float32)
        gsend[part(i)] = total.astype(gsend.dtype)

    for i in range(early // 2, early):
        arrived(i)

    @pl.when(z < late)
    def _():
        hear_answers()
        for d in range(1, n_z):
            z_copy(d, z).start()

    weight_copies[3].wait()

    @pl.loop(0, chunks)
    def _(i):
        gown[part(i)] = jnp.dot(feat[part(i)], wgt[3], preferred_element_type=jnp.float32)

    @pl.when(relays & (z >= late))
    def _():
        seam_first(n_z - 1 - z).wait_recv()
        seam_second(n_z - 1 - z).start()

    arrived(chunks - 2)
    g_copy(0).start()

    for d in range(1, n_z):
        z_copy(d, (z + n_z - d) % n_z).wait_recv()
    for d in range(1, n_x):
        x_copy(d, x).start()

    arrived(chunks - 1)

    for i in range(1, chunks):
        g_copy(i).start()

    def forward(m):
        pair = xs[pl.ds(pl.multiple_of(m * block, block), 2 * block)]
        es[m] = jnp.dot(fwd[...], pair, preferred_element_type=jnp.float32)

    def products(first, last):
        more = first == 0

        @pl.loop(0, block // 8)
        def _(r):
            real = pl.ds(pl.multiple_of(r * 8, 8), 8)
            imag = pl.ds(pl.multiple_of(block + r * 8, 8), 8)
            for part_of in range(2):
                lanes = pl.ds(part_of * half, half)
                k_real = [kh[p, real, lanes] for p in range(blocks)]
                k_imag = [kh[p, imag, lanes] for p in range(blocks)]
                sum_real = [ys[a, real, lanes] if more and a else None for a in range(blocks)]
                sum_imag = [ys[a, imag, lanes] if more and a else None for a in range(blocks)]
                for m in range(first, last):
                    e_real, e_imag = es[m, real, lanes], es[m, imag, lanes]
                    for a in range(blocks):
                        p = blocks - 1 + a - m
                        if not 0 <= p < blocks:
                            continue
                        new_real = e_real * k_real[p] - e_imag * k_imag[p]
                        new_imag = e_imag * k_real[p] + e_real * k_imag[p]
                        if sum_real[a] is None:
                            sum_real[a], sum_imag[a] = new_real, new_imag
                        else:
                            sum_real[a] = sum_real[a] + new_real
                            sum_imag[a] = sum_imag[a] + new_imag
                for a in range(blocks):
                    if sum_real[a] is not None:
                        ys[a, real, lanes] = sum_real[a]
                        ys[a, imag, lanes] = sum_imag[a]

    def transform_taps():
        c_copy(1 - core).wait_recv()
        for p in range(blocks):
            pieces = []
            for seq in range(p * seqs, (p + 1) * seqs):
                at_core, at_x = seq % n_core, seq // n_core % n_x
                at_z, at_yh = seq // (n_core * n_x) % n_z, seq // (n_core * n_x * n_z)
                taps = kg[at_core, at_x, at_z, at_yh].astype(jnp.float32)
                pieces.append(jnp.concatenate([taps[:8], taps[8:]], 1))
            taps = jnp.concatenate(pieces, 0).astype(jnp.bfloat16)
            kh[p] = jnp.dot(fwd[:, :block], taps, preferred_element_type=jnp.float32)

    def transform_halo():
        done = 0
        for i in range(chunks):

            @pl.when(gets_halo)
            def _():
                h_copy(i).wait_recv()

            @pl.when(me == target)
            def _():
                for j in range(i * n_z // chunks, (i + 1) * n_z // chunks):
                    seam_second(j).wait_recv()

            ready = blocks if i == chunks - 1 else (i + 1) * blocks // chunks - 1
            pl.loop(done, ready)(forward)
            done = ready

    for copy in small_copies[1:]:
        copy.wait()
    pl.loop(blocks, 2 * blocks - 1)(forward)

    for d in range(1, n_x):
        x_copy(d, (x + n_x - d) % n_x).wait_recv()
    c_copy(core).start()

    @pl.when(relays & (z < late))
    def _():
        seam_first(n_z - 1 - z).wait_recv()
        seam_second(n_z - 1 - z).start()

    @pl.when(me == 0)
    def _():
        xs[pl.ds(0, rows)] = jnp.zeros((rows, channels), xs.dtype)

    def gate_of(i):
        g_copy(i).wait_recv()
        gate = gown[part(i)] + grecv[part(i)].astype(jnp.float32)
        return gate / (1.0 + jnp.exp(-gate))

    def gate_factor(i):
        gown[part(i)] = gate_of(i)

    taps_last = (z < late) & (me != target)

    @pl.when(taps_last)
    def _():
        transform_halo()
        transform_taps()
        products(blocks, 2 * blocks - 1)

    @pl.when(jnp.logical_not(taps_last))
    def _():
        transform_taps()
        products(blocks, 2 * blocks - 1)

        @pl.when(me == target)
        def _():
            pl.loop(0, chunks)(gate_factor)

        transform_halo()

    products(0, blocks)

    gain = skip[...]

    @pl.loop(0, blocks)
    def _(a):
        spectrum = ys[a].astype(jnp.bfloat16)
        back = jnp.dot(inv[...], spectrum, preferred_element_type=jnp.float32)
        direct = xs[pl.ds(pl.multiple_of(rows + a * block, block), block)].astype(jnp.float32)
        conv[pl.ds(pl.multiple_of(a * block, block), block)] = back + gain * direct

    @pl.when(me == target)
    def _():
        @pl.loop(0, chunks)
        def _(i):
            out[part(i)] = (conv[part(i)] * gown[part(i)]).astype(out.dtype)

    @pl.when(me != target)
    def _():
        @pl.loop(0, chunks)
        def _(i):
            out[part(i)] = (conv[part(i)] * gate_of(i)).astype(out.dtype)

    for i in range(chunks):
        v_copy(i).wait_send()
        g_copy(i).wait_send()

    @pl.when(sends_halo)
    def _():
        for i in range(chunks):
            h_copy(i).wait_send()

    a_copy(yh).wait_send()
    for d in range(1, n_z):
        z_copy(d, z).wait_send()
    for d in range(1, n_x):
        x_copy(d, x).wait_send()
    c_copy(core).wait_send()

    @pl.when(is_source)
    def _():
        for j in range(n_z):
            seam_first(j).wait_send()

    @pl.when(relays)
    def _():
        seam_second(n_z - 1 - z).wait_send()


def solution(mesh, grid=GRID, blocks=BLOCKS, chunks=CHUNKS):
    def on_device(features, value_weight, gate_weight, kernel, skip_gain):
        rows, depth = features.shape
        tap_rows, channels = kernel.shape
        block = rows // blocks
        fwd, inv = tables(block)
        f32, bf16 = jnp.float32, jnp.bfloat16
        dma = pltpu.SemaphoreType.DMA
        n_yh, n_z, n_x, n_core = grid
        return pl.pallas_call(
            functools.partial(layer, grid, blocks, chunks),
            out_shape=pltpu.VMEM((rows, channels), bf16),
            in_specs=[pl.BlockSpec(memory_space=pl.ANY)] * 7,
            out_specs=pl.BlockSpec(memory_space=pltpu.VMEM),
            scratch_shapes=[
                pltpu.VMEM((rows, depth), bf16),
                pltpu.VMEM((4, depth, channels), bf16),
                pltpu.VMEM((tap_rows, channels), bf16),
                pltpu.VMEM((1, channels), f32),
                pltpu.VMEM(fwd.shape, bf16),
                pltpu.VMEM(inv.shape, bf16),
                pltpu.VMEM((n_core, n_x, n_z, n_yh, 2 * tap_rows, channels // 2), bf16),
                pltpu.VMEM((rows, channels), WIRE),
                pltpu.VMEM((rows, channels), WIRE),
                pltpu.VMEM((rows, channels), WIRE),
                pltpu.VMEM((rows, channels), WIRE),
                pltpu.VMEM((rows, channels), f32),
                pltpu.VMEM((rows, channels), f32),
                pltpu.VMEM((2 * rows, channels), bf16),
                pltpu.VMEM((2 * blocks - 1, 2 * block, channels), f32),
                pltpu.VMEM((blocks, 2 * block, channels), f32),
                pltpu.VMEM((blocks, 2 * block, channels), f32),
                pltpu.VMEM((rows, channels), f32),
                pltpu.VMEM((rows // n_z, channels), bf16),
                dma((9,)),
                dma((chunks,)),
                dma((chunks,)),
                dma((chunks,)),
                dma((chunks,)),
                dma((chunks,)),
                dma((chunks,)),
                dma((chunks,)),
                dma((2,)),
                dma((n_z,)),
                dma((n_z,)),
                dma((n_x,)),
                dma((n_x,)),
                dma((2,)),
                dma((n_z,)),
                dma((2,)),
                dma((n_z,)),
            ],
            compiler_params=pltpu.CompilerParams(
                collective_id=0, has_side_effects=True, vmem_limit_bytes=56 * 2**20
            ),
            cost_estimate=pl.CostEstimate(
                flops=8 * rows * depth * channels,
                bytes_accessed=2 * (rows * depth + 4 * depth * channels + rows * channels),
                transcendentals=rows * channels,
            ),
        )(
            features,
            value_weight,
            gate_weight,
            kernel,
            skip_gain.reshape(1, channels),
            jnp.asarray(fwd),
            jnp.asarray(inv),
        )

    return jax.shard_map(
        on_device,
        mesh=mesh,
        in_specs=(P("seq", "ch"), P("ch", None), P("ch", None), P("seq", "ch"), P("ch")),
        out_specs=P("seq", "ch"),
        check_vma=False,
    )
```

```python
import functools
import math

import jax
import jax.numpy as jnp
import numpy as np
from jax import lax
from jax.experimental import pallas as pl
from jax.experimental.pallas import tpu as pltpu
from jax.sharding import PartitionSpec as P

MESH = pl.DeviceIdType.MESH
WIRE = jnp.bfloat16
GRID = (2, 8, 4, 2)
BLOCKS = 8
CHUNKS = 4


def tables(block):
    period = 2 * block
    freq = np.arange(block)[:, None] + 0.5
    place = np.arange(period)[None, :]
    phase = 2.0 * math.pi * freq * place / period
    forward = np.concatenate([np.cos(phase), np.sin(phase)], 0)
    inverse = forward.T[block:] * (2.0 / period)
    return forward.astype(jnp.bfloat16), inverse.astype(jnp.bfloat16)


def layer(
    grid,
    blocks,
    chunks,
    feat_hbm,
    vw_hbm,
    gw_hbm,
    ker_hbm,
    skip_hbm,
    fwd_hbm,
    inv_hbm,
    out,
    feat,
    wgt,
    ktmp,
    skip,
    fwd,
    inv,
    kg,
    vsend,
    vrecv,
    gsend,
    grecv,
    vown,
    gown,
    xs,
    es,
    kh,
    ys,
    conv,
    relay,
    in_sem,
    feat_sem,
    v_ssem,
    v_rsem,
    g_ssem,
    g_rsem,
    h_ssem,
    h_rsem,
    a_sem,
    z_ssem,
    z_rsem,
    x_ssem,
    x_rsem,
    c_sem,
    s_sem,
    r_sem,
    d_sem,
):
    n_yh, n_z, n_x, n_core = grid
    n_seq = n_yh * n_z * n_x * n_core
    rows = feat.shape[0]
    size = rows // chunks
    block = rows // blocks
    channels = vown.shape[1]
    seqs = n_seq // blocks

    me = lax.axis_index("seq")
    side = lax.axis_index("ch")
    core = me % n_core
    x = me // n_core % n_x
    z = me // (n_core * n_x) % n_z
    yh = me // (n_core * n_x * n_z)

    def seq_of(yh, z, x, core):
        return ((yh * n_z + z) * n_x + x) * n_core + core

    other = pl.ds(pl.multiple_of((1 - side) * channels, 128), channels)
    own = pl.ds(pl.multiple_of(side * channels, 128), channels)

    def feat_copy(i):
        part = pl.ds(pl.multiple_of(i * size, size), size)
        return pltpu.make_async_copy(feat_hbm.at[part], feat.at[part], feat_sem.at[i])

    weight_copies = [
        pltpu.make_async_copy(hbm.at[:, cols], wgt.at[j], in_sem.at[j])
        for j, (hbm, cols) in enumerate(
            ((vw_hbm, other), (vw_hbm, own), (gw_hbm, other), (gw_hbm, own))
        )
    ]
    small_copies = [
        pltpu.make_async_copy(hbm, ref, in_sem.at[4 + j])
        for j, (hbm, ref) in enumerate(
            (
                (ker_hbm, ktmp),
                (fwd_hbm, fwd),
                (inv_hbm, inv),
                (skip_hbm, skip),
            )
        )
    ]
    small_copies[0].start()
    feat_copy(0).start()
    weight_copies[0].start()
    for i in range(1, chunks):
        feat_copy(i).start()
    for copy in weight_copies[1:]:
        copy.start()
    for copy in small_copies[1:]:
        copy.start()

    partner = {"ch": 1 - side}
    following = {"seq": (me + 1) % n_seq}
    preceding = {"seq": (me + n_seq - 1) % n_seq}
    yh_partner = {"seq": seq_of(1 - yh, z, x, core)}
    core_partner = {"seq": seq_of(yh, z, x, 1 - core)}
    z_to = {d: {"seq": seq_of(yh, (z + d) % n_z, x, core)} for d in range(1, n_z)}
    x_to = {d: {"seq": seq_of(yh, z, (x + d) % n_x, core)} for d in range(1, n_x)}
    source, target = n_seq // 2 - 1, n_seq // 2
    at_end = (x == n_x - 1) & (core == n_core - 1)
    is_source = me == source
    direct = n_z // 2
    relays = at_end & (yh == 1)
    piece_rows = rows // n_z
    sends_halo = (me < n_seq - 1) & (me != source)
    gets_halo = (me > 0) & (me != target)

    late = n_z // 2
    others = [(z + d) % n_z for d in range(1, n_z)]
    z_devices = [{"seq": seq_of(yh, other, x, core)} for other in others]
    is_later = [(z < late) & (other > z) for other in others]
    is_earlier = [(other < late) & (other < z) for other in others]
    is_level = [(z >= late) & (other >= late) for other in others]
    leads = (core == n_core - 1) & sends_halo
    led = (core == 0) & gets_halo
    barrier = pltpu.get_barrier_semaphore()

    def signal(device):
        pl.semaphore_signal(barrier, inc=1, device_id=device, device_id_type=MESH)

    def signal_if(condition, device):
        @pl.when(condition)
        def _():
            signal(device)

    level = [partner, core_partner, yh_partner] + list(x_to.values())
    level_count = len(level)
    for device in level:
        signal(device)
    for device, condition in zip(z_devices, is_level):
        signal_if(condition, device)
    signal_if(led, preceding)

    @pl.when(me == target)
    def _():
        for j in range(n_z):
            signal({"seq": seq_of(1, j, n_x - 1, n_core - 1)})

    signal_if(relays | (me == target), {"seq": source})

    def count(*conditions):
        return sum(condition.astype(jnp.int32) for condition in conditions)

    def enter():
        pl.semaphore_wait(
            barrier,
            level_count
            + jnp.where(z < late, z, n_z - 1)
            + count(leads, relays)
            + jnp.where(is_source, n_z + 1, 0),
        )
        for device, later, earlier in zip(z_devices, is_later, is_earlier):
            signal_if(later | earlier, device)

    def hear_answers():
        pl.semaphore_wait(barrier, n_z - 1 - z)

    def remote(src, dst, ssem, rsem, device):
        return pltpu.make_async_remote_copy(
            src_ref=src,
            dst_ref=dst,
            send_sem=ssem,
            recv_sem=rsem,
            device_id=device,
            device_id_type=MESH,
        )

    def part(i):
        return pl.ds(pl.multiple_of(i * size, size), size)

    def v_copy(i):
        return remote(vsend.at[part(i)], vrecv.at[part(i)], v_ssem.at[i], v_rsem.at[i], partner)

    def g_copy(i):
        return remote(gsend.at[part(i)], grecv.at[part(i)], g_ssem.at[i], g_rsem.at[i], partner)

    def current(i):
        return pl.ds(pl.multiple_of(rows + i * size, size), size)

    def h_copy(i):
        return remote(xs.at[current(i)], xs.at[part(i)], h_ssem.at[i], h_rsem.at[i], following)

    def piece(j, start):
        return pl.ds(pl.multiple_of(start + j * piece_rows, piece_rows), piece_rows)

    def seam_direct(j):
        return remote(
            xs.at[piece(j, rows)], xs.at[piece(j, 0)], s_sem.at[j], d_sem.at[j], {"seq": target}
        )

    def seam_first(j):
        device = {"seq": seq_of(1, n_z - 1 - j, n_x - 1, n_core - 1)}
        return remote(xs.at[piece(j, rows)], relay, s_sem.at[j], r_sem.at[0], device)

    def seam_second(j):
        return remote(relay, xs.at[piece(j, 0)], r_sem.at[1], d_sem.at[j], {"seq": target})

    def a_copy(sender):
        slot = kg.at[core, x, z, sender]
        return remote(slot, slot, a_sem.at[0], a_sem.at[1], yh_partner)

    def z_copy(d, sender):
        slot = kg.at[core, x, sender]
        return remote(slot, slot, z_ssem.at[d], z_rsem.at[d], z_to[d])

    def x_copy(d, sender):
        slot = kg.at[core, sender]
        return remote(slot, slot, x_ssem.at[d], x_rsem.at[d], x_to[d])

    def c_copy(sender):
        slot = kg.at[sender]
        return remote(slot, slot, c_sem.at[0], c_sem.at[1], core_partner)

    small_copies[0].wait()
    taps = ktmp[...].astype(jnp.float32)
    half = channels // 2
    kg[core, x, z, yh] = jnp.concatenate([taps[:, :half], taps[:, half:]], 0).astype(kg.dtype)

    weight_copies[0].wait()

    @pl.loop(0, chunks)
    def _(i):
        feat_copy(i).wait()
        total = jnp.dot(feat[part(i)], wgt[0], preferred_element_type=jnp.float32)
        vsend[part(i)] = total.astype(vsend.dtype)

        @pl.when(i == 0)
        def _():
            enter()
            a_copy(yh).start()

        v_copy(i).start()

    def arrived(i):
        v_copy(i).wait_recv()
        total = vown[part(i)] + vrecv[part(i)].astype(jnp.float32)
        xs[current(i)] = total.astype(xs.dtype)

        @pl.when(sends_halo)
        def _():
            h_copy(i).start()

        @pl.when(is_source)
        def _():
            for j in range(i * n_z // chunks, (i + 1) * n_z // chunks):
                (seam_first(j) if j < direct else seam_direct(j)).start()

    a_copy(1 - yh).wait_recv()

    @pl.when(z >= late)
    def _():
        for d in range(1, n_z):
            z_copy(d, z).start()

    weight_copies[1].wait()

    @pl.loop(0, chunks)
    def _(i):
        vown[part(i)] = jnp.dot(feat[part(i)], wgt[1], preferred_element_type=jnp.float32)

    early = chunks - 2
    for i in range(early // 2):
        arrived(i)

    weight_copies[2].wait()

    @pl.loop(0, chunks)
    def _(i):
        total = jnp.dot(feat[part(i)], wgt[2], preferred_element_type=jnp.float32)
        gsend[part(i)] = total.astype(gsend.dtype)

    for i in range(early // 2, early):
        arrived(i)

    @pl.when(z < late)
    def _():
        hear_answers()
        for d in range(1, n_z):
            z_copy(d, z).start()

    weight_copies[3].wait()

    @pl.loop(0, chunks)
    def _(i):
        gown[part(i)] = jnp.dot(feat[part(i)], wgt[3], preferred_element_type=jnp.float32)

    @pl.when(relays & (z >= late) & (n_z - 1 - z < direct))
    def _():
        seam_first(n_z - 1 - z).wait_recv()
        seam_second(n_z - 1 - z).start()

    arrived(chunks - 2)
    g_copy(0).start()

    for d in range(1, n_z):
        z_copy(d, (z + n_z - d) % n_z).wait_recv()
    for d in range(1, n_x):
        x_copy(d, x).start()

    arrived(chunks - 1)

    for i in range(1, chunks):
        g_copy(i).start()

    def forward(m):
        pair = xs[pl.ds(pl.multiple_of(m * block, block), 2 * block)]
        es[m] = jnp.dot(fwd[...], pair, preferred_element_type=jnp.float32)

    def products(first, last):
        more = first == 0

        @pl.loop(0, block // 8)
        def _(r):
            real = pl.ds(pl.multiple_of(r * 8, 8), 8)
            imag = pl.ds(pl.multiple_of(block + r * 8, 8), 8)
            for part_of in range(2):
                lanes = pl.ds(part_of * half, half)
                k_real = [kh[p, real, lanes] for p in range(blocks)]
                k_imag = [kh[p, imag, lanes] for p in range(blocks)]
                sum_real = [ys[a, real, lanes] if more and a else None for a in range(blocks)]
                sum_imag = [ys[a, imag, lanes] if more and a else None for a in range(blocks)]
                for m in range(first, last):
                    e_real, e_imag = es[m, real, lanes], es[m, imag, lanes]
                    for a in range(blocks):
                        p = blocks - 1 + a - m
                        if not 0 <= p < blocks:
                            continue
                        new_real = e_real * k_real[p] - e_imag * k_imag[p]
                        new_imag = e_imag * k_real[p] + e_real * k_imag[p]
                        if sum_real[a] is None:
                            sum_real[a], sum_imag[a] = new_real, new_imag
                        else:
                            sum_real[a] = sum_real[a] + new_real
                            sum_imag[a] = sum_imag[a] + new_imag
                for a in range(blocks):
                    if sum_real[a] is not None:
                        ys[a, real, lanes] = sum_real[a]
                        ys[a, imag, lanes] = sum_imag[a]

    def transform_taps():
        c_copy(1 - core).wait_recv()
        for p in range(blocks):
            pieces = []
            for seq in range(p * seqs, (p + 1) * seqs):
                at_core, at_x = seq % n_core, seq // n_core % n_x
                at_z, at_yh = seq // (n_core * n_x) % n_z, seq // (n_core * n_x * n_z)
                taps = kg[at_core, at_x, at_z, at_yh].astype(jnp.float32)
                pieces.append(jnp.concatenate([taps[:8], taps[8:]], 1))
            taps = jnp.concatenate(pieces, 0).astype(jnp.bfloat16)
            kh[p] = jnp.dot(fwd[:, :block], taps, preferred_element_type=jnp.float32)

    def transform_halo():
        done = 0
        for i in range(chunks):

            @pl.when(gets_halo)
            def _():
                h_copy(i).wait_recv()

            @pl.when(me == target)
            def _():
                for j in range(i * n_z // chunks, (i + 1) * n_z // chunks):
                    (seam_second(j) if j < direct else seam_direct(j)).wait_recv()

            ready = blocks if i == chunks - 1 else (i + 1) * blocks // chunks - 1
            pl.loop(done, ready)(forward)
            done = ready

    for copy in small_copies[1:]:
        copy.wait()
    pl.loop(blocks, 2 * blocks - 1)(forward)

    for d in range(1, n_x):
        x_copy(d, (x + n_x - d) % n_x).wait_recv()
    c_copy(core).start()

    @pl.when(relays & (z < late) & (n_z - 1 - z < direct))
    def _():
        seam_first(n_z - 1 - z).wait_recv()
        seam_second(n_z - 1 - z).start()

    @pl.when(me == 0)
    def _():
        xs[pl.ds(0, rows)] = jnp.zeros((rows, channels), xs.dtype)

    def gate_of(i):
        g_copy(i).wait_recv()
        gate = gown[part(i)] + grecv[part(i)].astype(jnp.float32)
        return gate / (1.0 + jnp.exp(-gate))

    def gate_factor(i):
        gown[part(i)] = gate_of(i)

    taps_last = (z < late) & (me != target)

    @pl.when(taps_last)
    def _():
        transform_halo()
        transform_taps()
        products(blocks, 2 * blocks - 1)

    @pl.when(jnp.logical_not(taps_last))
    def _():
        transform_taps()
        products(blocks, 2 * blocks - 1)

        @pl.when(me == target)
        def _():
            pl.loop(0, chunks)(gate_factor)

        transform_halo()

    products(0, blocks)

    gain = skip[...]

    @pl.loop(0, blocks)
    def _(a):
        spectrum = ys[a].astype(jnp.bfloat16)
        back = jnp.dot(inv[...], spectrum, preferred_element_type=jnp.float32)
        direct = xs[pl.ds(pl.multiple_of(rows + a * block, block), block)].astype(jnp.float32)
        conv[pl.ds(pl.multiple_of(a * block, block), block)] = back + gain * direct

    @pl.when(me == target)
    def _():
        @pl.loop(0, chunks)
        def _(i):
            out[part(i)] = (conv[part(i)] * gown[part(i)]).astype(out.dtype)

    @pl.when(me != target)
    def _():
        @pl.loop(0, chunks)
        def _(i):
            out[part(i)] = (conv[part(i)] * gate_of(i)).astype(out.dtype)

    for i in range(chunks):
        v_copy(i).wait_send()
        g_copy(i).wait_send()

    @pl.when(sends_halo)
    def _():
        for i in range(chunks):
            h_copy(i).wait_send()

    a_copy(yh).wait_send()
    for d in range(1, n_z):
        z_copy(d, z).wait_send()
    for d in range(1, n_x):
        x_copy(d, x).wait_send()
    c_copy(core).wait_send()

    @pl.when(is_source)
    def _():
        for j in range(n_z):
            (seam_first(j) if j < direct else seam_direct(j)).wait_send()

    @pl.when(relays & (n_z - 1 - z < direct))
    def _():
        seam_second(n_z - 1 - z).wait_send()


def solution(mesh, grid=GRID, blocks=BLOCKS, chunks=CHUNKS):
    def on_device(features, value_weight, gate_weight, kernel, skip_gain):
        rows, depth = features.shape
        tap_rows, channels = kernel.shape
        block = rows // blocks
        fwd, inv = tables(block)
        f32, bf16 = jnp.float32, jnp.bfloat16
        dma = pltpu.SemaphoreType.DMA
        n_yh, n_z, n_x, n_core = grid
        return pl.pallas_call(
            functools.partial(layer, grid, blocks, chunks),
            out_shape=pltpu.VMEM((rows, channels), bf16),
            in_specs=[pl.BlockSpec(memory_space=pl.ANY)] * 7,
            out_specs=pl.BlockSpec(memory_space=pltpu.VMEM),
            scratch_shapes=[
                pltpu.VMEM((rows, depth), bf16),
                pltpu.VMEM((4, depth, channels), bf16),
                pltpu.VMEM((tap_rows, channels), bf16),
                pltpu.VMEM((1, channels), f32),
                pltpu.VMEM(fwd.shape, bf16),
                pltpu.VMEM(inv.shape, bf16),
                pltpu.VMEM((n_core, n_x, n_z, n_yh, 2 * tap_rows, channels // 2), bf16),
                pltpu.VMEM((rows, channels), WIRE),
                pltpu.VMEM((rows, channels), WIRE),
                pltpu.VMEM((rows, channels), WIRE),
                pltpu.VMEM((rows, channels), WIRE),
                pltpu.VMEM((rows, channels), f32),
                pltpu.VMEM((rows, channels), f32),
                pltpu.VMEM((2 * rows, channels), bf16),
                pltpu.VMEM((2 * blocks - 1, 2 * block, channels), f32),
                pltpu.VMEM((blocks, 2 * block, channels), f32),
                pltpu.VMEM((blocks, 2 * block, channels), f32),
                pltpu.VMEM((rows, channels), f32),
                pltpu.VMEM((rows // n_z, channels), bf16),
                dma((9,)),
                dma((chunks,)),
                dma((chunks,)),
                dma((chunks,)),
                dma((chunks,)),
                dma((chunks,)),
                dma((chunks,)),
                dma((chunks,)),
                dma((2,)),
                dma((n_z,)),
                dma((n_z,)),
                dma((n_x,)),
                dma((n_x,)),
                dma((2,)),
                dma((n_z,)),
                dma((2,)),
                dma((n_z,)),
            ],
            compiler_params=pltpu.CompilerParams(
                collective_id=0, has_side_effects=True, vmem_limit_bytes=56 * 2**20
            ),
            cost_estimate=pl.CostEstimate(
                flops=8 * rows * depth * channels,
                bytes_accessed=2 * (rows * depth + 4 * depth * channels + rows * channels),
                transcendentals=rows * channels,
            ),
        )(
            features,
            value_weight,
            gate_weight,
            kernel,
            skip_gain.reshape(1, channels),
            jnp.asarray(fwd),
            jnp.asarray(inv),
        )

    return jax.shard_map(
        on_device,
        mesh=mesh,
        in_specs=(P("seq", "ch"), P("ch", None), P("ch", None), P("seq", "ch"), P("ch")),
        out_specs=P("seq", "ch"),
        check_vma=False,
    )
```

```python
import functools
import math

import jax
import jax.numpy as jnp
import numpy as np
from jax import lax
from jax.experimental import pallas as pl
from jax.experimental.pallas import tpu as pltpu
from jax.sharding import PartitionSpec as P

MESH = pl.DeviceIdType.MESH
WIRE = jnp.bfloat16
GRID = (2, 8, 4, 2)
BLOCKS = 8
CHUNKS = 4


def tables(block):
    period = 2 * block
    freq = np.arange(block)[:, None] + 0.5
    place = np.arange(period)[None, :]
    phase = 2.0 * math.pi * freq * place / period
    forward = np.concatenate([np.cos(phase), np.sin(phase)], 0)
    inverse = forward.T[block:] * (2.0 / period)
    return forward.astype(jnp.bfloat16), inverse.astype(jnp.bfloat16)


def layer(
    grid,
    blocks,
    chunks,
    feat_hbm,
    vw_hbm,
    gw_hbm,
    ker_hbm,
    skip_hbm,
    fwd_hbm,
    inv_hbm,
    out,
    feat,
    wgt,
    ktmp,
    skip,
    fwd,
    inv,
    kg,
    vsend,
    vrecv,
    gsend,
    grecv,
    vown,
    gown,
    xs,
    es,
    kh,
    ys,
    conv,
    relay,
    in_sem,
    feat_sem,
    v_ssem,
    v_rsem,
    g_ssem,
    g_rsem,
    h_ssem,
    h_rsem,
    a_sem,
    z_ssem,
    z_rsem,
    x_ssem,
    x_rsem,
    c_sem,
    s_sem,
    r_sem,
    d_sem,
):
    n_yh, n_z, n_x, n_core = grid
    n_seq = n_yh * n_z * n_x * n_core
    rows = feat.shape[0]
    size = rows // chunks
    block = rows // blocks
    channels = vown.shape[1]
    seqs = n_seq // blocks

    me = lax.axis_index("seq")
    side = lax.axis_index("ch")
    core = me % n_core
    x = me // n_core % n_x
    z = me // (n_core * n_x) % n_z
    yh = me // (n_core * n_x * n_z)

    def seq_of(yh, z, x, core):
        return ((yh * n_z + z) * n_x + x) * n_core + core

    other = pl.ds(pl.multiple_of((1 - side) * channels, 128), channels)
    own = pl.ds(pl.multiple_of(side * channels, 128), channels)

    def feat_copy(i):
        part = pl.ds(pl.multiple_of(i * size, size), size)
        return pltpu.make_async_copy(feat_hbm.at[part], feat.at[part], feat_sem.at[i])

    weight_copies = [
        pltpu.make_async_copy(hbm.at[:, cols], wgt.at[j], in_sem.at[j])
        for j, (hbm, cols) in enumerate(
            ((vw_hbm, other), (vw_hbm, own), (gw_hbm, other), (gw_hbm, own))
        )
    ]
    small_copies = [
        pltpu.make_async_copy(hbm, ref, in_sem.at[4 + j])
        for j, (hbm, ref) in enumerate(
            (
                (ker_hbm, ktmp),
                (fwd_hbm, fwd),
                (inv_hbm, inv),
                (skip_hbm, skip),
            )
        )
    ]
    small_copies[0].start()
    feat_copy(0).start()
    weight_copies[0].start()
    for i in range(1, chunks):
        feat_copy(i).start()
    for copy in weight_copies[1:]:
        copy.start()
    for copy in small_copies[1:]:
        copy.start()

    partner = {"ch": 1 - side}
    following = {"seq": (me + 1) % n_seq}
    preceding = {"seq": (me + n_seq - 1) % n_seq}
    yh_partner = {"seq": seq_of(1 - yh, z, x, core)}
    core_partner = {"seq": seq_of(yh, z, x, 1 - core)}
    z_to = {d: {"seq": seq_of(yh, (z + d) % n_z, x, core)} for d in range(1, n_z)}
    x_to = {d: {"seq": seq_of(yh, z, (x + d) % n_x, core)} for d in range(1, n_x)}
    source, target = n_seq // 2 - 1, n_seq // 2
    at_end = (x == n_x - 1) & (core == n_core - 1)
    is_source = me == source
    direct = n_z // 2
    relays = at_end & (yh == 1)
    piece_rows = rows // n_z
    sends_halo = (me < n_seq - 1) & (me != source)
    gets_halo = (me > 0) & (me != target)

    late = n_z // 2
    others = [(z + d) % n_z for d in range(1, n_z)]
    z_devices = [{"seq": seq_of(yh, other, x, core)} for other in others]
    is_later = [(z < late) & (other > z) for other in others]
    is_earlier = [(other < late) & (other < z) for other in others]
    is_level = [(z >= late) & (other >= late) for other in others]
    leads = (core == n_core - 1) & sends_halo
    led = (core == 0) & gets_halo
    barrier = pltpu.get_barrier_semaphore()

    def signal(device):
        pl.semaphore_signal(barrier, inc=1, device_id=device, device_id_type=MESH)

    def signal_if(condition, device):
        @pl.when(condition)
        def _():
            signal(device)

    level = [partner, core_partner, yh_partner] + list(x_to.values())
    level_count = len(level)
    for device in level:
        signal(device)
    for device, condition in zip(z_devices, is_level):
        signal_if(condition, device)
    signal_if(led, preceding)

    @pl.when(me == target)
    def _():
        for j in range(n_z):
            signal({"seq": seq_of(1, j, n_x - 1, n_core - 1)})

    signal_if(relays | (me == target), {"seq": source})

    def count(*conditions):
        return sum(condition.astype(jnp.int32) for condition in conditions)

    def enter():
        pl.semaphore_wait(
            barrier,
            level_count
            + jnp.where(z < late, z, n_z - 1)
            + count(leads, relays)
            + jnp.where(is_source, n_z + 1, 0),
        )
        for device, later, earlier in zip(z_devices, is_later, is_earlier):
            signal_if(later | earlier, device)

    def hear_answers():
        pl.semaphore_wait(barrier, n_z - 1 - z)

    def remote(src, dst, ssem, rsem, device):
        return pltpu.make_async_remote_copy(
            src_ref=src,
            dst_ref=dst,
            send_sem=ssem,
            recv_sem=rsem,
            device_id=device,
            device_id_type=MESH,
        )

    def part(i):
        return pl.ds(pl.multiple_of(i * size, size), size)

    def v_copy(i):
        return remote(vsend.at[part(i)], vrecv.at[part(i)], v_ssem.at[i], v_rsem.at[i], partner)

    def g_copy(i):
        return remote(gsend.at[part(i)], grecv.at[part(i)], g_ssem.at[i], g_rsem.at[i], partner)

    def current(i):
        return pl.ds(pl.multiple_of(rows + i * size, size), size)

    def h_copy(i):
        return remote(xs.at[current(i)], xs.at[part(i)], h_ssem.at[i], h_rsem.at[i], following)

    def piece(j, start):
        return pl.ds(pl.multiple_of(start + j * piece_rows, piece_rows), piece_rows)

    def seam_direct(j):
        return remote(
            xs.at[piece(j, rows)], xs.at[piece(j, 0)], s_sem.at[j], d_sem.at[j], {"seq": target}
        )

    def seam_first(j):
        device = {"seq": seq_of(1, n_z - 1 - j, n_x - 1, n_core - 1)}
        return remote(xs.at[piece(j, rows)], relay, s_sem.at[j], r_sem.at[0], device)

    def seam_second(j):
        return remote(relay, xs.at[piece(j, 0)], r_sem.at[1], d_sem.at[j], {"seq": target})

    def a_copy(sender):
        slot = kg.at[core, x, z, sender]
        return remote(slot, slot, a_sem.at[0], a_sem.at[1], yh_partner)

    def z_copy(d, sender):
        slot = kg.at[core, x, sender]
        return remote(slot, slot, z_ssem.at[d], z_rsem.at[d], z_to[d])

    def x_copy(d, sender):
        slot = kg.at[core, sender]
        return remote(slot, slot, x_ssem.at[d], x_rsem.at[d], x_to[d])

    def c_copy(sender):
        slot = kg.at[sender]
        return remote(slot, slot, c_sem.at[0], c_sem.at[1], core_partner)

    small_copies[0].wait()
    taps = ktmp[...].astype(jnp.float32)
    half = channels // 2
    kg[core, x, z, yh] = jnp.concatenate([taps[:, :half], taps[:, half:]], 0).astype(kg.dtype)

    weight_copies[0].wait()

    @pl.loop(0, chunks)
    def _(i):
        feat_copy(i).wait()
        total = jnp.dot(feat[part(i)], wgt[0], preferred_element_type=jnp.float32)
        vsend[part(i)] = total.astype(vsend.dtype)

        @pl.when(i == 0)
        def _():
            enter()
            a_copy(yh).start()

        v_copy(i).start()

    def arrived(i):
        v_copy(i).wait_recv()
        total = vown[part(i)] + vrecv[part(i)].astype(jnp.float32)
        xs[current(i)] = total.astype(xs.dtype)

        @pl.when(sends_halo)
        def _():
            h_copy(i).start()

        @pl.when(is_source)
        def _():
            for j in range(i * n_z // chunks, (i + 1) * n_z // chunks):
                (seam_first(j) if j < direct else seam_direct(j)).start()

    a_copy(1 - yh).wait_recv()

    @pl.when(z >= late)
    def _():
        for d in range(1, n_z):
            z_copy(d, z).start()

    weight_copies[1].wait()

    @pl.loop(0, chunks)
    def _(i):
        vown[part(i)] = jnp.dot(feat[part(i)], wgt[1], preferred_element_type=jnp.float32)

    early = chunks - 2
    for i in range(early // 2):
        arrived(i)

    weight_copies[2].wait()

    @pl.loop(0, chunks)
    def _(i):
        total = jnp.dot(feat[part(i)], wgt[2], preferred_element_type=jnp.float32)
        gsend[part(i)] = total.astype(gsend.dtype)

    @pl.when(z < late)
    def _():
        hear_answers()
        for d in range(1, n_z):
            z_copy(d, z).start()

    for i in range(early // 2, early):
        arrived(i)

    weight_copies[3].wait()

    @pl.loop(0, chunks)
    def _(i):
        gown[part(i)] = jnp.dot(feat[part(i)], wgt[3], preferred_element_type=jnp.float32)

    @pl.when(relays & (z >= late) & (n_z - 1 - z < direct))
    def _():
        seam_first(n_z - 1 - z).wait_recv()
        seam_second(n_z - 1 - z).start()

    arrived(chunks - 2)
    g_copy(0).start()

    for d in range(1, n_z):
        z_copy(d, (z + n_z - d) % n_z).wait_recv()
    for d in range(1, n_x):
        x_copy(d, x).start()

    arrived(chunks - 1)

    for i in range(1, chunks):
        g_copy(i).start()

    def forward(m):
        pair = xs[pl.ds(pl.multiple_of(m * block, block), 2 * block)]
        es[m] = jnp.dot(fwd[...], pair, preferred_element_type=jnp.float32)

    def products(first, last):
        more = first == 0

        @pl.loop(0, block // 8)
        def _(r):
            real = pl.ds(pl.multiple_of(r * 8, 8), 8)
            imag = pl.ds(pl.multiple_of(block + r * 8, 8), 8)
            for part_of in range(2):
                lanes = pl.ds(part_of * half, half)
                k_real = [kh[p, real, lanes] for p in range(blocks)]
                k_imag = [kh[p, imag, lanes] for p in range(blocks)]
                sum_real = [ys[a, real, lanes] if more and a else None for a in range(blocks)]
                sum_imag = [ys[a, imag, lanes] if more and a else None for a in range(blocks)]
                for m in range(first, last):
                    e_real, e_imag = es[m, real, lanes], es[m, imag, lanes]
                    for a in range(blocks):
                        p = blocks - 1 + a - m
                        if not 0 <= p < blocks:
                            continue
                        new_real = e_real * k_real[p] - e_imag * k_imag[p]
                        new_imag = e_imag * k_real[p] + e_real * k_imag[p]
                        if sum_real[a] is None:
                            sum_real[a], sum_imag[a] = new_real, new_imag
                        else:
                            sum_real[a] = sum_real[a] + new_real
                            sum_imag[a] = sum_imag[a] + new_imag
                for a in range(blocks):
                    if sum_real[a] is not None:
                        ys[a, real, lanes] = sum_real[a]
                        ys[a, imag, lanes] = sum_imag[a]

    def transform_taps():
        c_copy(1 - core).wait_recv()
        for p in range(blocks):
            pieces = []
            for seq in range(p * seqs, (p + 1) * seqs):
                at_core, at_x = seq % n_core, seq // n_core % n_x
                at_z, at_yh = seq // (n_core * n_x) % n_z, seq // (n_core * n_x * n_z)
                taps = kg[at_core, at_x, at_z, at_yh].astype(jnp.float32)
                pieces.append(jnp.concatenate([taps[:8], taps[8:]], 1))
            taps = jnp.concatenate(pieces, 0).astype(jnp.bfloat16)
            kh[p] = jnp.dot(fwd[:, :block], taps, preferred_element_type=jnp.float32)

    def transform_halo():
        done = 0
        for i in range(chunks):

            @pl.when(gets_halo)
            def _():
                h_copy(i).wait_recv()

            @pl.when(me == target)
            def _():
                for j in range(i * n_z // chunks, (i + 1) * n_z // chunks):
                    (seam_second(j) if j < direct else seam_direct(j)).wait_recv()

            ready = blocks if i == chunks - 1 else (i + 1) * blocks // chunks - 1
            pl.loop(done, ready)(forward)
            done = ready

    for copy in small_copies[1:]:
        copy.wait()
    pl.loop(blocks, 2 * blocks - 1)(forward)

    for d in range(1, n_x):
        x_copy(d, (x + n_x - d) % n_x).wait_recv()
    c_copy(core).start()

    @pl.when(relays & (z < late) & (n_z - 1 - z < direct))
    def _():
        seam_first(n_z - 1 - z).wait_recv()
        seam_second(n_z - 1 - z).start()

    @pl.when(me == 0)
    def _():
        xs[pl.ds(0, rows)] = jnp.zeros((rows, channels), xs.dtype)

    def gate_of(i):
        g_copy(i).wait_recv()
        gate = gown[part(i)] + grecv[part(i)].astype(jnp.float32)
        return gate / (1.0 + jnp.exp(-gate))

    def gate_factor(i):
        gown[part(i)] = gate_of(i)

    taps_last = (z < late) & (me != target)

    @pl.when(taps_last)
    def _():
        transform_halo()
        transform_taps()
        products(blocks, 2 * blocks - 1)

    @pl.when(jnp.logical_not(taps_last))
    def _():
        transform_taps()
        products(blocks, 2 * blocks - 1)

        @pl.when(me == target)
        def _():
            pl.loop(0, chunks)(gate_factor)

        transform_halo()

    products(0, blocks)

    gain = skip[...]

    @pl.loop(0, blocks)
    def _(a):
        spectrum = ys[a].astype(jnp.bfloat16)
        back = jnp.dot(inv[...], spectrum, preferred_element_type=jnp.float32)
        direct = xs[pl.ds(pl.multiple_of(rows + a * block, block), block)].astype(jnp.float32)
        conv[pl.ds(pl.multiple_of(a * block, block), block)] = back + gain * direct

    @pl.when(me == target)
    def _():
        @pl.loop(0, chunks)
        def _(i):
            out[part(i)] = (conv[part(i)] * gown[part(i)]).astype(out.dtype)

    @pl.when(me != target)
    def _():
        @pl.loop(0, chunks)
        def _(i):
            out[part(i)] = (conv[part(i)] * gate_of(i)).astype(out.dtype)

    for i in range(chunks):
        v_copy(i).wait_send()
        g_copy(i).wait_send()

    @pl.when(sends_halo)
    def _():
        for i in range(chunks):
            h_copy(i).wait_send()

    a_copy(yh).wait_send()
    for d in range(1, n_z):
        z_copy(d, z).wait_send()
    for d in range(1, n_x):
        x_copy(d, x).wait_send()
    c_copy(core).wait_send()

    @pl.when(is_source)
    def _():
        for j in range(n_z):
            (seam_first(j) if j < direct else seam_direct(j)).wait_send()

    @pl.when(relays & (n_z - 1 - z < direct))
    def _():
        seam_second(n_z - 1 - z).wait_send()


def solution(mesh, grid=GRID, blocks=BLOCKS, chunks=CHUNKS):
    def on_device(features, value_weight, gate_weight, kernel, skip_gain):
        rows, depth = features.shape
        tap_rows, channels = kernel.shape
        block = rows // blocks
        fwd, inv = tables(block)
        f32, bf16 = jnp.float32, jnp.bfloat16
        dma = pltpu.SemaphoreType.DMA
        n_yh, n_z, n_x, n_core = grid
        return pl.pallas_call(
            functools.partial(layer, grid, blocks, chunks),
            out_shape=pltpu.VMEM((rows, channels), bf16),
            in_specs=[pl.BlockSpec(memory_space=pl.ANY)] * 7,
            out_specs=pl.BlockSpec(memory_space=pltpu.VMEM),
            scratch_shapes=[
                pltpu.VMEM((rows, depth), bf16),
                pltpu.VMEM((4, depth, channels), bf16),
                pltpu.VMEM((tap_rows, channels), bf16),
                pltpu.VMEM((1, channels), f32),
                pltpu.VMEM(fwd.shape, bf16),
                pltpu.VMEM(inv.shape, bf16),
                pltpu.VMEM((n_core, n_x, n_z, n_yh, 2 * tap_rows, channels // 2), bf16),
                pltpu.VMEM((rows, channels), WIRE),
                pltpu.VMEM((rows, channels), WIRE),
                pltpu.VMEM((rows, channels), WIRE),
                pltpu.VMEM((rows, channels), WIRE),
                pltpu.VMEM((rows, channels), f32),
                pltpu.VMEM((rows, channels), f32),
                pltpu.VMEM((2 * rows, channels), bf16),
                pltpu.VMEM((2 * blocks - 1, 2 * block, channels), f32),
                pltpu.VMEM((blocks, 2 * block, channels), f32),
                pltpu.VMEM((blocks, 2 * block, channels), f32),
                pltpu.VMEM((rows, channels), f32),
                pltpu.VMEM((rows // n_z, channels), bf16),
                dma((9,)),
                dma((chunks,)),
                dma((chunks,)),
                dma((chunks,)),
                dma((chunks,)),
                dma((chunks,)),
                dma((chunks,)),
                dma((chunks,)),
                dma((2,)),
                dma((n_z,)),
                dma((n_z,)),
                dma((n_x,)),
                dma((n_x,)),
                dma((2,)),
                dma((n_z,)),
                dma((2,)),
                dma((n_z,)),
            ],
            compiler_params=pltpu.CompilerParams(
                collective_id=0, has_side_effects=True, vmem_limit_bytes=56 * 2**20
            ),
            cost_estimate=pl.CostEstimate(
                flops=8 * rows * depth * channels,
                bytes_accessed=2 * (rows * depth + 4 * depth * channels + rows * channels),
                transcendentals=rows * channels,
            ),
        )(
            features,
            value_weight,
            gate_weight,
            kernel,
            skip_gain.reshape(1, channels),
            jnp.asarray(fwd),
            jnp.asarray(inv),
        )

    return jax.shard_map(
        on_device,
        mesh=mesh,
        in_specs=(P("seq", "ch"), P("ch", None), P("ch", None), P("seq", "ch"), P("ch")),
        out_specs=P("seq", "ch"),
        check_vma=False,
    )
```
